512 devices in a mesh: copy: 32 (over y, z_lo, core), fsdp: 16 (over x, z_hi).
Axes of the slice: x: 4, y: 4, z: 16 (z_hi: 4, z_lo: 4; z = z_hi * 4 + z_lo), core: 2. Of those that a mesh axis runs over, the one named last changes fastest.
Arguments:
- hidden: bfloat16 [32, 512, 2048], P('copy', 'fsdp'), may hold values from -6 to 6, as said below
- gain: float32 [32, 2048], P('copy'), may hold values from 0.5 to 1.5
- head_weight: bfloat16 [32, 2048, 16384], P('copy', None, 'fsdp'), may hold values from -3.3766065 to 3.3766065
- targets: int32 [512], replicated, may hold values from 0 to 16383
- partner: int32 [32], replicated, may hold values from 0 to 31, each once
Outputs:
- gain_gradient: float32 [32, 2048], P('copy', 'fsdp')
- token_loss: float32 [32, 512], P('copy', 'fsdp')
The draws below stay inside these ranges and needn't reach their ends.
Inputs may be any that keep to these rules, and one draw needn't show every extreme that they name: hidden states of order one.
All inputs are finite; a program needn't handle non-finite values.
Results may differ from the reference program's by a relative error of at most 0.013.
Values may be sent and summed in bfloat16 or wider, within the bound.
A program may use at most 64 MiB of HBM per device.

```python
import math
import jax
import jax.numpy as jnp
import numpy as np
from jax import lax

D = 2048
VOCAB = 16384
TOKENS = 512
COPIES = 32


def base_field(key):
    return jnp.clip(jax.random.normal(key, (COPIES, TOKENS, D), jnp.float32), -6.0, 6.0)


def draw_hidden(key, part):
    shared = base_field(key)
    return shared.astype(jnp.bfloat16)


def draw_head_weight(key, part):
    key = jax.random.fold_in(key, 23)
    key_main = jax.random.fold_in(key, 0)
    key_common = jax.random.fold_in(key, 3)
    output_weight = jnp.clip(jax.random.normal(key_main, (COPIES, D, VOCAB), jnp.float32), -6.0, 6.0) * (2.0 / D ** 0.5)
    common = jnp.clip(jax.random.normal(key_common, (COPIES, D, 1), jnp.float32), -6.0, 6.0) * (6.0 / D ** 0.5)
    return (output_weight + common).astype(jnp.bfloat16)


def with_ends(result, key, least, high):
    longest = result.shape.index(max(result.shape))
    spots = []
    for shift in (0, 1):
        where = [jax.random.randint(jax.random.fold_in(key, axis), (), 0, length) for axis, length in enumerate(result.shape)]
        where[longest] = (where[longest] + shift) % result.shape[longest]
        spots.append(tuple(where))
    return result.at[spots[0]].set(least).at[spots[1]].set(high)


def cumulative_ranks(number_of, skew):
    weights = [(1 << 20) // math.isqrt(grade ** skew) + 1 for grade in range(1, number_of + 1)]
    width = 1 + sum(weights) // (1 << 30)
    return np.cumsum(np.array([max(1, weight // width) for weight in weights]))


def ranked(stream_key, shape, number_of, lean):
    listing = cumulative_ranks(number_of, lean)
    lot = jax.random.randint(jax.random.fold_in(stream_key, 1), shape, 0, int(listing[number_of - 1]))
    rank = jnp.searchsorted(jnp.asarray(listing, jnp.int32), lot, side="right")
    return jax.random.permutation(jax.random.fold_in(stream_key, 2), number_of)[rank].astype(jnp.int32)


def setup_inputs(seed: int = 0) -> dict:
    key_of = jax.random.split(jax.random.key(seed), 6)
    hidden = draw_hidden(jax.random.fold_in(key_of[5], 71), 0)
    gain = jnp.clip(1.0 + 0.1 * jax.random.normal(key_of[1], (COPIES, D), jnp.float32), 0.5, 1.5)
    head_weight = draw_head_weight(jax.random.fold_in(key_of[5], 71), 0)
    targets = with_ends(ranked(key_of[3], (TOKENS,), VOCAB, 2), jax.random.fold_in(key_of[3], 3), 0, VOCAB - 1).astype(jnp.int32)
    partner = jax.random.permutation(key_of[4], COPIES).astype(jnp.int32)
    return {"hidden": hidden, "gain": gain, "head_weight": head_weight, "targets": targets, "partner": partner}


distill_weight = 0.5
stability_offset = 1e-05

def apply_final_norm(input_rows, inverse_root_scale):
    value_list = input_rows.astype(jnp.float32)
    centered_input = value_list * lax.rsqrt(lax.optimization_barrier(jnp.mean(value_list * value_list, axis=-1, keepdims=True)) + stability_offset)
    normalized_rows = (centered_input * inverse_root_scale[None, :]).astype(jnp.bfloat16)
    return (centered_input, normalized_rows)

def forward_hidden_rows(input_rows, inverse_root_scale, output_weight):
    centered_input, normalized_rows = apply_final_norm(input_rows, inverse_root_scale)
    output_scores = jnp.dot(normalized_rows, output_weight, preferred_element_type=jnp.float32)
    return (centered_input, jax.nn.log_softmax(output_scores, axis=-1))

def reference(hidden, gain, head_weight, targets, partner):
    sent_all = lax.map(lambda triple: forward_hidden_rows(*triple)[1].astype(jnp.bfloat16), (hidden, gain, head_weight))
    partner_sent = jnp.take(sent_all, partner.astype(jnp.int32), axis=0)
    vocab_ids = jnp.arange(VOCAB, dtype=jnp.int32)
    onehot = (targets.astype(jnp.int32)[:, None] == vocab_ids[None, :]).astype(jnp.float32)

    def per_copy(quad):
        input_rows, inverse_root_scale, output_weight, other = quad
        centered_input, log_probability = forward_hidden_rows(input_rows, inverse_root_scale, output_weight)
        partner_logq = other.astype(jnp.float32)
        partner_q = jnp.exp(partner_logq)
        prob = jnp.exp(log_probability)
        token_loss = -lax.optimization_barrier(jnp.sum(onehot * log_probability, axis=-1)) + distill_weight * lax.optimization_barrier(jnp.sum(partner_q * (partner_logq - log_probability), axis=-1))
        q_total = lax.optimization_barrier(jnp.sum(partner_q, axis=-1, keepdims=True))
        dlogits = (prob - onehot + distill_weight * (q_total * prob - partner_q)).astype(jnp.bfloat16)
        normalized_gradient = lax.dot_general(dlogits, output_weight, (((1,), (1,)), ((), ())), preferred_element_type=jnp.float32)
        gain_gradient = lax.optimization_barrier(jnp.sum(centered_input * normalized_gradient, axis=0))
        return (gain_gradient, token_loss)
    gain_gradient, token_loss = lax.map(per_copy, (hidden, gain, head_weight, partner_sent))
    return (gain_gradient, token_loss)
```

```python
import functools

import jax
import jax.numpy as jnp
from jax import lax
from jax.experimental import pallas as pl
from jax.experimental.pallas import tpu as pltpu
from jax.sharding import PartitionSpec as P

MESH = pl.DeviceIdType.MESH
F32, BF16 = jnp.float32, jnp.bfloat16
WEIGHT = 0.5
OFFSET = 1e-05
RING = 4
ROWS = 16
HALVES = 2
BLOCK = 256
LANES = 128


def column_of(row):
    return jnp.broadcast_to(row, (LANES, LANES)).T


def kernel(
    copies, shards, hidden, gain, w_hbm, targets, partner, gg_out, tl_out,
    w, hid, xhat, normed, logp, dlog, lse_col, q_col, t_col, loss_col, gacc,
    stat_src, stat_buf, qs_src, qs_buf, qc_src, qc_buf, fin_src, fin_buf,
    stage1, buf1_first, buf1_second, stage2, buf2,
    w_sem, z_send, z_recv, x_send, x_recv, s_send, s_recv, qs_send, qs_recv, qc_send, qc_recv,
    f_send, f_recv, p1_send, p1_recv, p2_send, p2_recv,
):
    buf1 = (buf1_first, buf1_second)
    me_c, me_f = lax.axis_index("copy"), lax.axis_index("fsdp")
    me_x, me_z = me_f // RING, lax.rem(me_f, RING)
    vocab = w.shape[1]
    depth = w.shape[0]
    half_tokens = shards * ROWS
    piece_rows, piece_cols = stage1.shape[2], stage1.shape[3]
    splits = vocab // piece_cols

    load_w = pltpu.make_async_copy(w_hbm, w, w_sem)
    load_w.start()

    barrier = pltpu.get_barrier_semaphore()

    def greet_copy(k, carry):
        pl.semaphore_signal(barrier, inc=1, device_id=(lax.rem(me_c + k, copies), me_f), device_id_type=MESH)
        return carry

    def greet_shard(k, carry):
        pl.semaphore_signal(barrier, inc=1, device_id=(me_c, lax.rem(me_f + k, shards)), device_id_type=MESH)
        return carry

    lax.fori_loop(1, shards, greet_shard, 0)
    lax.fori_loop(1, copies, greet_copy, 0)
    for half in range(HALVES):
        hid[me_f, half] = hidden[half * ROWS : (half + 1) * ROWS, :]
    pl.semaphore_wait(barrier, copies + shards - 2)

    def shard_of(dx, dz):
        return lax.rem(me_x + dx + RING, RING) * RING + lax.rem(me_z + dz + RING, RING)

    def hop(which, half, to, send, recv):
        return pltpu.make_async_remote_copy(
            src_ref=hid.at[which, half], dst_ref=hid.at[which, half], send_sem=send, recv_sem=recv,
            device_id=(me_c, to), device_id_type=MESH,
        )

    def z_copy(half, slot):
        onward = 1 - 2 * half
        dz, to = ((0, onward), (0, -onward), (-onward, onward))[slot]
        return hop(shard_of(0, dz), half, shard_of(0, to), z_send.at[half * 3 + slot], z_recv.at[half * 3 + slot])

    def z_offset(half, slot):
        onward = 1 - 2 * half
        return (-onward, onward, -2 * onward)[slot]

    def x_copy(half, order, slot):
        onward = 1 - 2 * half
        dz = 0 if order == 0 else z_offset(half, order - 1)
        dx, to = ((0, onward), (0, -onward), (-onward, onward))[slot]
        at = (half * RING + order) * 3 + slot
        return hop(shard_of(dx, dz), half, shard_of(to, 0), x_send.at[at], x_recv.at[at])

    def spread(half, order):
        x_copy(half, order, 0).start()
        x_copy(half, order, 1).start()

    def pass_on(half, order):
        x_copy(half, order, 0).wait_recv()
        x_copy(half, order, 2).start()

    def gather_start(half):
        z_copy(half, 0).start()
        z_copy(half, 1).start()
        spread(half, 0)

    def gather_first(half):
        pass_on(half, 0)
        z_copy(half, 0).wait_recv()
        z_copy(half, 2).start()
        spread(half, 1)
        z_copy(half, 1).wait_recv()
        spread(half, 2)

    def gather_second(half):
        pass_on(half, 1)
        pass_on(half, 2)
        z_copy(half, 2).wait_recv()
        spread(half, 3)
        pass_on(half, 3)

    def gather_end(half):
        for order in range(RING):
            x_copy(half, order, 1).wait_recv()
            x_copy(half, order, 2).wait_recv()

    def to_all(axis, src_of, buf, send, recv):
        size = copies if axis == "copy" else shards

        def step(k, carry):
            if axis == "copy":
                peer = lax.rem(me_c + k, size)
                device = (peer, me_f)
            else:
                peer = lax.rem(me_f + k, size)
                device = (me_c, peer)
            pltpu.make_async_remote_copy(
                src_ref=src_of(peer, k), dst_ref=buf.at[k], send_sem=send, recv_sem=recv,
                device_id=device, device_id_type=MESH,
            ).start()
            return carry

        lax.fori_loop(1, size, step, 0)

    def wait_all(buf, sem):
        rest = buf.at[pl.ds(1, buf.shape[0] - 1)]
        pltpu.make_async_copy(rest, rest, sem).wait()

    def normalise(half):
        def step(s, carry):
            rows = pl.ds(pl.multiple_of(half * half_tokens + s * ROWS, ROWS), ROWS)
            value = hid[s, half].astype(F32)
            scale = lax.rsqrt(jnp.mean(value * value, axis=-1, keepdims=True) + OFFSET)
            unit = value * scale
            xhat[rows, :] = unit
            normed[rows, :] = (unit * gain[...]).astype(BF16)
            return carry

        lax.fori_loop(0, shards, step, 0)

    def head(half):
        rows = pl.ds(half * half_tokens, half_tokens)

        def step(b, carry):
            cols = pl.ds(pl.multiple_of(b * BLOCK, BLOCK), BLOCK)
            logp[rows, cols] = jnp.dot(normed[rows, :], w[:, cols], preferred_element_type=F32)
            return carry

        lax.fori_loop(0, vocab // BLOCK, step, 0)

        def total(s, carry):
            at = pl.ds(pl.multiple_of(half * half_tokens + s * ROWS, ROWS), ROWS)
            value = logp[at, :]
            top = jnp.max(value, axis=-1, keepdims=True)
            local = top + jnp.log(jnp.sum(jnp.exp(value - top), axis=-1, keepdims=True))
            lse_col[at, :] = jnp.broadcast_to(local, (ROWS, LANES))
            return carry

        lax.fori_loop(0, shards, total, 0)
        for part in range(half_tokens // LANES):
            at = pl.ds(half * half_tokens + part * LANES, LANES)
            stat_src[half, part : part + 1, :] = lse_col[at, :].T[0:1, :]
        stat_buf[half, 0] = stat_src[half]
        to_all("fsdp", lambda peer, k: stat_src.at[half], stat_buf.at[half], s_send.at[half], s_recv.at[half])

    def log_probability(half):
        wait_all(stat_buf.at[half], s_recv.at[half])
        parts = stat_buf[half]
        top = jnp.max(parts, axis=0)
        lse = top + jnp.log(jnp.sum(jnp.exp(parts - top[None]), axis=0))
        for part in range(half_tokens // LANES):
            at = pl.ds(half * half_tokens + part * LANES, LANES)
            lse_col[at, :] = column_of(lse[part : part + 1, :])

        def step(s, carry):
            at = pl.ds(pl.multiple_of(half * half_tokens + s * ROWS, ROWS), ROWS)
            value = logp[at, :] - lse_col[at, 0:1]
            logp[at, :] = value
            rounded = value.astype(BF16)
            first = (s * ROWS) // piece_rows * splits
            inner = pl.ds(pl.multiple_of(lax.rem(s * ROWS, piece_rows), ROWS), ROWS)
            for split in range(splits):
                stage1[half, first + split, inner, :] = rounded[:, split * piece_cols : (split + 1) * piece_cols]
            part = jnp.sum(jnp.exp(rounded.astype(F32)), axis=-1, keepdims=True)
            q_col[at, :] = jnp.broadcast_to(part, (ROWS, LANES))
            return carry

        lax.fori_loop(0, shards, step, 0)

    def exchange_first(half):
        to_all("copy", lambda peer, k: stage1.at[half, peer], buf1[half], p1_send.at[half], p1_recv.at[half])
        buf1[half][0] = stage1[half, me_c]

    def exchange_second(half):
        wait_all(buf1[half], p1_recv.at[half])

        def pick(j, carry):
            source = partner[lax.rem(me_c + j, copies)]
            stage2[half, j] = buf1[half][lax.rem(me_c - source + copies, copies)]
            return carry

        lax.fori_loop(0, copies, pick, 0)
        to_all("copy", lambda peer, k: stage2.at[half, k], buf2.at[half], p2_send.at[half], p2_recv.at[half])
        buf2[half, 0] = stage2[half, 0]

    def totals_first():
        for part in range(HALVES * half_tokens // LANES):
            qs_src[part : part + 1, :] = q_col[part * LANES : (part + 1) * LANES, :].T[0:1, :]
        qs_buf[0] = qs_src[...]
        to_all("fsdp", lambda peer, k: qs_src, qs_buf, qs_send.at[0], qs_recv.at[0])

    def totals_second():
        wait_all(qs_buf, qs_recv.at[0])
        qc_src[...] = jnp.sum(qs_buf[...], axis=0)
        qc_buf[0] = qc_src[...]
        to_all("copy", lambda peer, k: qc_src, qc_buf, qc_send.at[0], qc_recv.at[0])

    def totals_third():
        wait_all(qc_buf, qc_recv.at[0])
        mine = qc_buf[lax.rem(me_c - partner[me_c] + copies, copies)]
        for part in range(HALVES * half_tokens // LANES):
            q_col[part * LANES : (part + 1) * LANES, :] = column_of(mine[part : part + 1, :])

    def backward(half):
        wait_all(buf2.at[half], p2_recv.at[half])
        base = me_f * vocab

        def step(s, carry):
            at = pl.ds(pl.multiple_of(half * half_tokens + s * ROWS, ROWS), ROWS)
            here = pl.ds(pl.multiple_of(s * ROWS, ROWS), ROWS)
            token = pl.ds(pl.multiple_of(s * (HALVES * ROWS) + half * ROWS, ROWS), ROWS)
            first = (s * ROWS) // piece_rows * splits
            inner = pl.ds(pl.multiple_of(lax.rem(s * ROWS, piece_rows), ROWS), ROWS)
            q_total = q_col[at, 0:1]
            target = t_col[token, 0:1]
            loss = jnp.zeros((ROWS, 1), F32)
            for split in range(splits):
                cols = slice(split * piece_cols, (split + 1) * piece_cols)
                slot = lax.rem(me_c - (first + split) + copies, copies)
                logq = buf2[half, slot, inner, :].astype(F32)
                q = jnp.exp(logq)
                value = logp[at, cols]
                prob = jnp.exp(value)
                ids = base + split * piece_cols + lax.broadcasted_iota(jnp.int32, (ROWS, piece_cols), 1)
                hot = ids == target
                term = WEIGHT * (q * (logq - value)) - jnp.where(hot, value, 0.0)
                loss = loss + jnp.sum(term, axis=-1, keepdims=True)
                slope = prob - jnp.where(hot, 1.0, 0.0) + WEIGHT * (q_total * prob - q)
                dlog[here, cols] = slope.astype(BF16)
            loss_col[token, :] = jnp.broadcast_to(loss, (ROWS, LANES))
            return carry

        lax.fori_loop(0, shards, step, 0)
        rows = pl.ds(half * half_tokens, half_tokens)

        def product(b, carry):
            at = pl.ds(pl.multiple_of(b * BLOCK, BLOCK), BLOCK)
            piece = lax.dot_general(
                dlog[...], w[at, :], (((1,), (1,)), ((), ())), preferred_element_type=F32
            )
            part = jnp.sum(xhat[rows, at] * piece, axis=0, keepdims=True)
            if half == 0:
                gacc[:, at] = part
            else:
                gacc[:, at] = gacc[:, at] + part
            return carry

        lax.fori_loop(0, depth // BLOCK, product, 0)

    gather_start(0)
    stat_src[...] = jnp.zeros_like(stat_src)
    qs_src[...] = jnp.zeros_like(qs_src)
    fin_src[...] = jnp.zeros_like(fin_src)
    for part in range(HALVES * half_tokens // LANES):
        at = pl.ds(part * LANES, LANES)
        row = targets[part : part + 1, :]
        t_col[at, :] = column_of(row)
    gather_first(0)
    z_copy(1, 0).start()
    gather_second(0)
    z_copy(1, 1).start()
    spread(1, 0)
    gather_end(0)
    normalise(0)
    load_w.wait()
    head(0)
    gather_first(1)
    log_probability(0)
    exchange_first(0)
    gather_second(1)
    gather_end(1)
    normalise(1)
    head(1)
    log_probability(1)
    exchange_first(1)
    totals_first()
    exchange_second(0)
    totals_second()
    exchange_second(1)
    totals_third()
    backward(0)
    backward(1)

    per_row = LANES // (HALVES * ROWS)
    for part in range(shards // per_row):
        row = loss_col[part * LANES : (part + 1) * LANES, :].T[0:1, :]
        for j in range(part * per_row, (part + 1) * per_row):
            fin_src[j, 0:1, :] = gacc[:, j * LANES : (j + 1) * LANES]
            fin_src[j, 1:2, :] = row
    to_all("fsdp", lambda peer, k: fin_src.at[peer], fin_buf, f_send.at[0], f_recv.at[0])
    fin_buf[0] = fin_src[me_f]

    for half in range(HALVES):
        for slot in range(3):
            z_copy(half, slot).wait_send()
            for order in range(RING):
                x_copy(half, order, slot).wait_send()
        wait_all(stat_buf.at[half], s_send.at[half])
        wait_all(buf1[half], p1_send.at[half])
        wait_all(buf2.at[half], p2_send.at[half])
    wait_all(qs_buf, qs_send.at[0])
    wait_all(qc_buf, qc_send.at[0])
    wait_all(fin_buf, f_send.at[0])

    wait_all(fin_buf, f_recv.at[0])
    whole = jnp.sum(fin_buf[...], axis=0)
    gg_out[...] = whole[0:1, :]
    wide = HALVES * ROWS
    row = whole[1:2, :]
    result = row[:, 0:wide]
    for k in range(1, per_row):
        result = jnp.where(lax.rem(me_f, per_row) == k, row[:, k * wide : (k + 1) * wide], result)
    tl_out[...] = result


def per_device(copies, shards, hidden, gain, head_weight, targets, partner):
    mine, depth = hidden.shape[1], hidden.shape[2]
    vocab = head_weight.shape[2]
    tokens = mine * shards
    half_tokens = tokens // HALVES
    groups = min(half_tokens // ROWS, copies)
    piece = (half_tokens // groups, vocab // (copies // groups))
    vmem = pl.BlockSpec(memory_space=pltpu.VMEM)
    dma = pltpu.SemaphoreType.DMA
    return pl.pallas_call(
        functools.partial(kernel, copies, shards),
        out_shape=(
            jax.ShapeDtypeStruct((1, depth // shards), F32),
            jax.ShapeDtypeStruct((1, mine), F32),
        ),
        in_specs=[vmem, vmem, pl.BlockSpec(memory_space=pl.ANY), vmem, pl.BlockSpec(memory_space=pltpu.SMEM)],
        out_specs=(vmem, vmem),
        scratch_shapes=[
            pltpu.VMEM((depth, vocab), BF16),
            pltpu.VMEM((shards, HALVES, ROWS, depth), BF16),
            pltpu.VMEM((tokens, depth), F32),
            pltpu.VMEM((tokens, depth), BF16),
            pltpu.VMEM((tokens, vocab), F32),
            pltpu.VMEM((half_tokens, vocab), BF16),
            pltpu.VMEM((tokens, LANES), F32),
            pltpu.VMEM((tokens, LANES), F32),
            pltpu.VMEM((tokens, LANES), jnp.int32),
            pltpu.VMEM((tokens, LANES), F32),
            pltpu.VMEM((1, depth), F32),
            pltpu.VMEM((HALVES, 8, LANES), F32),
            pltpu.VMEM((HALVES, shards, 8, LANES), F32),
            pltpu.VMEM((8, LANES), F32),
            pltpu.VMEM((shards, 8, LANES), F32),
            pltpu.VMEM((8, LANES), F32),
            pltpu.VMEM((copies, 8, LANES), F32),
            pltpu.VMEM((shards, 8, LANES), F32),
            pltpu.VMEM((shards, 8, LANES), F32),
        ]
        + [
            pltpu.VMEM((HALVES, copies) + piece, BF16),
            pltpu.VMEM((copies,) + piece, BF16),
            pltpu.VMEM((copies,) + piece, BF16),
            pltpu.VMEM((HALVES, copies) + piece, BF16),
            pltpu.VMEM((HALVES, copies) + piece, BF16),
        ]
        + [
            dma,
            dma((HALVES * 3,)),
            dma((HALVES * 3,)),
            dma((HALVES * RING * 3,)),
            dma((HALVES * RING * 3,)),
            dma((HALVES,)),
            dma((HALVES,)),
        ]
        + [dma((1,))] * 6
        + [dma((HALVES,))] * 4,
        compiler_params=pltpu.CompilerParams(
            collective_id=0, has_side_effects=True, vmem_limit_bytes=48 * 1024 * 1024
        ),
        cost_estimate=pl.CostEstimate(
            flops=4 * tokens * depth * vocab,
            bytes_accessed=2 * depth * vocab,
            transcendentals=4 * tokens * vocab,
        ),
    )(hidden[0], gain, head_weight[0], targets.reshape(-1, LANES), partner)


def solution(mesh):
    in_specs = (P("copy", "fsdp", None), P("copy", None), P("copy", None, "fsdp"), P(), P())
    out_specs = (P("copy", "fsdp"), P("copy", "fsdp"))
    return jax.shard_map(
        functools.partial(per_device, mesh.shape["copy"], mesh.shape["fsdp"]),
        mesh=mesh, in_specs=in_specs, out_specs=out_specs, check_vma=False,
    )
```

```python
import functools

import jax
import jax.numpy as jnp
from jax import lax
from jax.experimental import pallas as pl
from jax.experimental.pallas import tpu as pltpu
from jax.sharding import PartitionSpec as P

MESH = pl.DeviceIdType.MESH
F32, BF16 = jnp.float32, jnp.bfloat16
WEIGHT = 0.5
OFFSET = 1e-05
RING = 4
CHUNKS = RING
ROWS = 16
BLOCK = 256
LANES = 128


def column_of(row):
    return jnp.broadcast_to(row, (LANES, LANES)).T


def kernel(
    copies, shards, hidden_in, gain_in, w_in, targets_in, partner_in, gg_out, tl_out,
    w, hid, gain, targets, partner, xhat, normed, logits, dlog, stat_col, t_col, loss_col, turned, gacc,
    sx_src, sx_buf, sz_src, sz_buf, cq_src, cq_buf, fin_src, fin_buf,
    stage1, buf1_0, buf1_1, buf1_2, buf1_3, stage2, buf2,
    in_sem, z_send, z_recv, x_send, x_recv, sx_send, sx_recv, sz_send, sz_recv, cq_send, cq_recv, f_send, f_recv,
    p1_send, p1_recv, p2_send, p2_recv,
):
    buf1 = (buf1_0, buf1_1, buf1_2, buf1_3)
    me_c, me_f = lax.axis_index("copy"), lax.axis_index("fsdp")
    me_x, me_z = me_f // RING, lax.rem(me_f, RING)
    depth, vocab = w.shape
    share = hid.shape[1]
    half_share = share // 2
    tokens = share * RING
    piece_rows, piece_cols = stage1.shape[2], stage1.shape[3]
    splits = vocab // piece_cols

    loads = [
        pltpu.make_async_copy(source, target, in_sem.at[i])
        for i, (source, target) in enumerate(
            ((hidden_in, hid.at[me_f]), (partner_in, partner), (targets_in, targets), (gain_in, gain), (w_in, w))
        )
    ]
    for load in loads:
        load.start()

    barrier = pltpu.get_barrier_semaphore()

    def greet_copy(k, carry):
        pl.semaphore_signal(barrier, inc=1, device_id=(lax.rem(me_c + k, copies), me_f), device_id_type=MESH)
        return carry

    def greet_shard(k, carry):
        pl.semaphore_signal(barrier, inc=1, device_id=(me_c, lax.rem(me_f + k, shards)), device_id_type=MESH)
        return carry

    lax.fori_loop(1, shards, greet_shard, 0)
    lax.fori_loop(1, copies, greet_copy, 0)
    sx_src[...] = jnp.zeros_like(sx_src)
    fin_src[...] = jnp.zeros_like(fin_src)
    turned[...] = jnp.zeros_like(turned)
    for load in loads[:3]:
        load.wait()
    for part in range(CHUNKS * tokens // LANES):
        t_col[part * LANES : (part + 1) * LANES, :] = column_of(targets[part : part + 1, :])
    pl.semaphore_wait(barrier, copies + shards - 2)

    def shard_of(dx, dz):
        return lax.rem(me_x + dx + RING, RING) * RING + lax.rem(me_z + dz + RING, RING)

    def hop(which, half, to, send, recv):
        rows = pl.ds(half * half_share, half_share)
        return pltpu.make_async_remote_copy(
            src_ref=hid.at[which, rows], dst_ref=hid.at[which, rows], send_sem=send, recv_sem=recv,
            device_id=(me_c, to), device_id_type=MESH,
        )

    def z_copy(half, slot):
        onward = 1 - 2 * half
        dz, to = ((0, onward), (0, -onward), (-onward, onward))[slot]
        at = half * 3 + slot
        return hop(shard_of(0, dz), half, shard_of(0, to), z_send.at[at], z_recv.at[at])

    CHUNK_Z = (0, -1, 1, 2)

    def x_copy(half, chunk, slot):
        onward = 1 - 2 * half
        dx, to = ((0, onward), (0, -onward), (-onward, onward))[slot]
        at = (half * CHUNKS + chunk) * 3 + slot
        return hop(shard_of(dx, CHUNK_Z[chunk]), half, shard_of(to, 0), x_send.at[at], x_recv.at[at])

    def spread(half, chunk):
        x_copy(half, chunk, 0).start()
        x_copy(half, chunk, 1).start()

    def pass_on(chunk):
        for half in (0, 1):
            x_copy(half, chunk, 0).wait_recv()
            x_copy(half, chunk, 2).start()

    def gather_end(chunk):
        for half in (0, 1):
            x_copy(half, chunk, 1).wait_recv()
            x_copy(half, chunk, 2).wait_recv()

    def to_all(axis, src_of, buf, send, recv):
        size = buf.shape[0]

        def step(k, carry):
            if axis == "copy":
                peer = lax.rem(me_c + k, size)
                device = (peer, me_f)
            elif axis == "fsdp":
                peer = lax.rem(me_f + k, size)
                device = (me_c, peer)
            elif axis == "x":
                peer = shard_of(k, 0)
                device = (me_c, peer)
            else:
                peer = shard_of(0, k)
                device = (me_c, peer)
            pltpu.make_async_remote_copy(
                src_ref=src_of(peer, k), dst_ref=buf.at[k], send_sem=send, recv_sem=recv,
                device_id=device, device_id_type=MESH,
            ).start()
            return carry

        lax.fori_loop(1, size, step, 0)

    def wait_all(buf, sem):
        rest = buf.at[pl.ds(1, buf.shape[0] - 1)]
        pltpu.make_async_copy(rest, rest, sem).wait()

    def chunk_z(chunk):
        return lax.rem(me_z + CHUNK_Z[chunk] + RING, RING)

    def rows_of(z, g):
        return pl.ds(pl.multiple_of(z * tokens + g * ROWS, ROWS), ROWS)

    def place(g):
        first = (g * ROWS) // piece_rows * splits
        return first, pl.ds(pl.multiple_of(lax.rem(g * ROWS, piece_rows), ROWS), ROWS)

    groups = tokens // ROWS
    lane = lax.broadcasted_iota(jnp.int32, (ROWS, LANES), 1)

    def forward(chunk):
        z = chunk_z(chunk)

        def normalise(g, carry):
            at = rows_of(z, g)
            inside = pl.ds(pl.multiple_of(lax.rem(g * ROWS, share), ROWS), ROWS)
            value = hid[(g * ROWS) // share * RING + z, inside, :].astype(F32)
            scale = lax.rsqrt(jnp.mean(value * value, axis=-1, keepdims=True) + OFFSET)
            unit = value * scale
            xhat[at, :] = unit
            normed[at, :] = (unit * gain[...]).astype(BF16)
            return carry

        lax.fori_loop(0, groups, normalise, 0, unroll=2)
        rows = pl.ds(pl.multiple_of(z * tokens, tokens), tokens)

        def product(b, carry):
            cols = pl.ds(pl.multiple_of(b * BLOCK, BLOCK), BLOCK)
            logits[rows, cols] = jnp.dot(normed[rows, :], w[:, cols], preferred_element_type=F32)
            return carry

        lax.fori_loop(0, vocab // BLOCK, product, 0)

        def rounded(g, carry):
            at = rows_of(z, g)
            value = logits[at, :]
            top = jnp.max(value, axis=-1, keepdims=True)
            stat_col[at, :] = jnp.broadcast_to(top, (ROWS, LANES))
            short = (value - top).astype(BF16)
            first, inner = place(g)
            for split in range(splits):
                stage1[chunk, first + split, inner, :] = short[:, split * piece_cols : (split + 1) * piece_cols]
            return carry

        lax.fori_loop(0, groups, rounded, 0, unroll=2)
        to_all("copy", lambda peer, k: stage1.at[chunk, peer], buf1[chunk], p1_send.at[chunk], p1_recv.at[chunk])
        buf1[chunk][0] = stage1[chunk, me_c]

    def sums(chunk):
        z = chunk_z(chunk)

        def step(g, carry):
            at = rows_of(z, g)
            top = stat_col[at, :]
            total = jnp.sum(jnp.exp(logits[at, :] - top[:, 0:1]), axis=-1, keepdims=True)
            first, inner = place(g)
            q_total = jnp.zeros((ROWS, 1), F32)
            for split in range(splits):
                short = stage1[chunk, first + split, inner, :].astype(F32)
                q_total = q_total + jnp.sum(jnp.exp(short), axis=-1, keepdims=True)
            stat_col[at, :] = jnp.where(lane == 0, top, jnp.where(lane == 1, total, q_total))
            return carry

        lax.fori_loop(0, groups, step, 0, unroll=2)
        flat = stat_col[pl.ds(pl.multiple_of(z * tokens, tokens), tokens), :].T
        for i in range(3):
            sx_src[:, pl.ds(pl.multiple_of(i * CHUNKS * LANES + z * LANES, LANES), LANES)] = flat[i : i + 1, :]

    def exchange_second(chunk):
        wait_all(buf1[chunk], p1_recv.at[chunk])

        def pick(j, carry):
            source = partner[lax.rem(me_c + j, copies)]
            stage2[chunk, j] = buf1[chunk][lax.rem(me_c - source + copies, copies)]
            return carry

        lax.fori_loop(0, copies, pick, 0)
        to_all("copy", lambda peer, k: stage2.at[chunk, k], buf2.at[chunk], p2_send.at[chunk], p2_recv.at[chunk])
        buf2[chunk, 0] = stage2[chunk, 0]

    wide = CHUNKS * LANES

    def joined(parts):
        tops = parts[:, :, 0:wide]
        top = jnp.max(tops, axis=0)
        factor = jnp.exp(tops - top[None])
        total = jnp.sum(parts[:, :, wide : 2 * wide] * factor, axis=0)
        q_total = jnp.sum(parts[:, :, 2 * wide : 3 * wide] * factor, axis=0)
        return top, total, q_total

    def statistics_x():
        sx_buf[0] = sx_src[...]
        to_all("x", lambda peer, k: sx_src, sx_buf, sx_send.at[0], sx_recv.at[0])

    def statistics_z():
        wait_all(sx_buf, sx_recv.at[0])
        for i, value in enumerate(joined(sx_buf[...])):
            sz_src[:, i * wide : (i + 1) * wide] = value
        sz_buf[0] = sz_src[...]
        to_all("z", lambda peer, k: sz_src, sz_buf, sz_send.at[0], sz_recv.at[0])

    def statistics_copy():
        wait_all(sz_buf, sz_recv.at[0])
        top, total, q_total = joined(sz_buf[...])
        log_total = jnp.log(total)
        cq_src[:, 0:wide] = (sx_src[:, 0:wide] - top) - log_total
        cq_src[:, wide : 2 * wide] = q_total / total
        cq_buf[0] = cq_src[...]
        to_all("copy", lambda peer, k: cq_src, cq_buf, cq_send.at[0], cq_recv.at[0])
        wait_all(sz_buf, sz_send.at[0])
        sz_src[:, 0:wide] = top
        sz_src[:, wide : 2 * wide] = log_total

    def statistics_end():
        wait_all(cq_buf, cq_recv.at[0])
        theirs = cq_buf[lax.rem(me_c - partner[me_c] + copies, copies)]
        for z in range(CHUNKS):
            at = slice(z * LANES, (z + 1) * LANES)
            turned[0:1, :] = sz_src[:, z * LANES : (z + 1) * LANES]
            turned[1:2, :] = sz_src[:, wide + z * LANES : wide + (z + 1) * LANES]
            turned[2:3, :] = theirs[:, z * LANES : (z + 1) * LANES]
            turned[3:4, :] = theirs[:, wide + z * LANES : wide + (z + 1) * LANES]
            stat_col[at, :] = turned[...].T

    def backward(chunk):
        wait_all(buf2.at[chunk], p2_recv.at[chunk])
        z = chunk_z(chunk)
        base = me_f * vocab

        def step(g, carry):
            at = rows_of(z, g)
            here = pl.ds(pl.multiple_of(g * ROWS, ROWS), ROWS)
            token = pl.ds(
                pl.multiple_of((g * ROWS) // share * tokens + z * share + lax.rem(g * ROWS, share), ROWS), ROWS
            )
            first, inner = place(g)
            top, log_total = stat_col[at, 0:1], stat_col[at, 1:2]
            lack, q_total = stat_col[at, 2:3], stat_col[at, 3:4]
            target = t_col[token, 0:1]
            loss = jnp.zeros((ROWS, 1), F32)
            for split in range(splits):
                cols = slice(split * piece_cols, (split + 1) * piece_cols)
                slot = lax.rem(me_c - (first + split) + copies, copies)
                logq = buf2[chunk, slot, inner, :].astype(F32) + lack
                q = jnp.exp(logq)
                value = (logits[at, cols] - top) - log_total
                prob = jnp.exp(value)
                ids = base + split * piece_cols + lax.broadcasted_iota(jnp.int32, (ROWS, piece_cols), 1)
                hot = ids == target
                term = WEIGHT * (q * (logq - value)) - jnp.where(hot, value, 0.0)
                loss = loss + jnp.sum(term, axis=-1, keepdims=True)
                slope = prob - jnp.where(hot, 1.0, 0.0) + WEIGHT * (q_total * prob - q)
                dlog[here, cols] = slope.astype(BF16)
            loss_col[token, :] = jnp.broadcast_to(loss, (ROWS, LANES))
            return carry

        lax.fori_loop(0, groups, step, 0, unroll=2)
        rows = pl.ds(pl.multiple_of(z * tokens, tokens), tokens)

        def product(b, carry):
            at = pl.ds(pl.multiple_of(b * BLOCK, BLOCK), BLOCK)
            piece = lax.dot_general(dlog[...], w[at, :], (((1,), (1,)), ((), ())), preferred_element_type=F32)
            part = jnp.sum(xhat[rows, at] * piece, axis=0, keepdims=True)
            if chunk == 0:
                gacc[:, at] = part
            else:
                gacc[:, at] = gacc[:, at] + part
            return carry

        lax.fori_loop(0, depth // BLOCK, product, 0)

    z_copy(0, 0).start()
    z_copy(1, 0).start()
    spread(0, 0)
    spread(1, 0)
    z_copy(0, 1).start()
    z_copy(1, 1).start()
    pass_on(0)
    loads[3].wait()
    loads[4].wait()
    gather_end(0)
    forward(0)
    z_copy(0, 0).wait_recv()
    z_copy(0, 2).start()
    spread(0, 1)
    z_copy(1, 0).wait_recv()
    z_copy(1, 2).start()
    spread(1, 2)
    z_copy(1, 1).wait_recv()
    spread(1, 1)
    z_copy(0, 1).wait_recv()
    spread(0, 2)
    sums(0)
    pass_on(1)
    pass_on(2)
    gather_end(1)
    forward(1)
    z_copy(0, 2).wait_recv()
    spread(0, 3)
    z_copy(1, 2).wait_recv()
    spread(1, 3)
    gather_end(2)
    forward(2)
    pass_on(3)
    exchange_second(0)
    gather_end(3)
    forward(3)
    for chunk in range(1, CHUNKS):
        sums(chunk)
    statistics_x()
    exchange_second(1)
    statistics_z()
    exchange_second(2)
    statistics_copy()
    exchange_second(3)
    statistics_end()
    for chunk in range(CHUNKS):
        backward(chunk)

    per_row = LANES // share
    for part in range(shards // per_row):
        row = loss_col[part * LANES : (part + 1) * LANES, :].T[0:1, :]
        for j in range(part * per_row, (part + 1) * per_row):
            fin_src[j, :, 0:LANES] = gacc[:, j * LANES : (j + 1) * LANES]
            fin_src[j, :, LANES : 2 * LANES] = row
    to_all("fsdp", lambda peer, k: fin_src.at[peer], fin_buf, f_send.at[0], f_recv.at[0])
    fin_buf[0] = fin_src[me_f]

    for half in (0, 1):
        for slot in range(3):
            z_copy(half, slot).wait_send()
            for chunk in range(CHUNKS):
                x_copy(half, chunk, slot).wait_send()
    for chunk in range(CHUNKS):
        wait_all(buf1[chunk], p1_send.at[chunk])
        wait_all(buf2.at[chunk], p2_send.at[chunk])
    wait_all(sx_buf, sx_send.at[0])
    wait_all(cq_buf, cq_send.at[0])
    wait_all(fin_buf, f_send.at[0])

    wait_all(fin_buf, f_recv.at[0])
    whole = jnp.sum(fin_buf[...], axis=0)
    gg_out[...] = whole[:, 0:LANES]
    row = whole[:, LANES : 2 * LANES]
    result = row[:, 0:share]
    for k in range(1, per_row):
        result = jnp.where(lax.rem(me_f, per_row) == k, row[:, k * share : (k + 1) * share], result)
    tl_out[...] = result


def per_device(copies, shards, hidden, gain, head_weight, targets, partner):
    share, depth = hidden.shape[1], hidden.shape[2]
    vocab = head_weight.shape[2]
    tokens = share * shards
    chunk = share * RING
    groups = min(chunk // ROWS, copies)
    piece = (chunk // groups, vocab // (copies // groups))
    anywhere, vmem = pl.BlockSpec(memory_space=pl.ANY), pl.BlockSpec(memory_space=pltpu.VMEM)
    dma = pltpu.SemaphoreType.DMA
    return pl.pallas_call(
        functools.partial(kernel, copies, shards),
        out_shape=(
            jax.ShapeDtypeStruct((1, depth // shards), F32),
            jax.ShapeDtypeStruct((1, share), F32),
        ),
        in_specs=[anywhere] * 5,
        out_specs=(vmem, vmem),
        scratch_shapes=[
            pltpu.VMEM((depth, vocab), BF16),
            pltpu.VMEM((shards, share, depth), BF16),
            pltpu.VMEM((1, depth), F32),
            pltpu.VMEM((tokens // LANES, LANES), jnp.int32),
            pltpu.SMEM((copies,), jnp.int32),
            pltpu.VMEM((tokens, depth), F32),
            pltpu.VMEM((tokens, depth), BF16),
            pltpu.VMEM((tokens, vocab), F32),
            pltpu.VMEM((chunk, vocab), BF16),
            pltpu.VMEM((tokens, LANES), F32),
            pltpu.VMEM((tokens, LANES), jnp.int32),
            pltpu.VMEM((tokens, LANES), F32),
            pltpu.VMEM((LANES, LANES), F32),
            pltpu.VMEM((1, depth), F32),
            pltpu.VMEM((1, 3 * tokens), F32),
            pltpu.VMEM((RING, 1, 3 * tokens), F32),
            pltpu.VMEM((1, 3 * tokens), F32),
            pltpu.VMEM((RING, 1, 3 * tokens), F32),
            pltpu.VMEM((1, 2 * tokens), F32),
            pltpu.VMEM((copies, 1, 2 * tokens), F32),
            pltpu.VMEM((shards, 1, 2 * LANES), F32),
            pltpu.VMEM((shards, 1, 2 * LANES), F32),
            pltpu.VMEM((CHUNKS, copies) + piece, BF16),
        ]
        + [pltpu.VMEM((copies,) + piece, BF16)] * CHUNKS
        + [pltpu.VMEM((CHUNKS, copies) + piece, BF16)] * 2
        + [
            dma((5,)),
            dma((2 * 3,)),
            dma((2 * 3,)),
            dma((2 * CHUNKS * 3,)),
            dma((2 * CHUNKS * 3,)),
        ]
        + [dma((1,))] * 8
        + [dma((CHUNKS,))] * 4,
        compiler_params=pltpu.CompilerParams(
            collective_id=0, has_side_effects=True, vmem_limit_bytes=56 * 1024 * 1024
        ),
        cost_estimate=pl.CostEstimate(
            flops=4 * tokens * depth * vocab,
            bytes_accessed=2 * depth * vocab,
            transcendentals=4 * tokens * vocab,
        ),
    )(hidden[0], gain, head_weight[0], targets.reshape(-1, LANES), partner)


def solution(mesh):
    in_specs = (P("copy", "fsdp", None), P("copy", None), P("copy", None, "fsdp"), P(), P())
    out_specs = (P("copy", "fsdp"), P("copy", "fsdp"))
    return jax.shard_map(
        functools.partial(per_device, mesh.shape["copy"], mesh.shape["fsdp"]),
        mesh=mesh, in_specs=in_specs, out_specs=out_specs, check_vma=False,
    )
```

```python
import functools

import jax
import jax.numpy as jnp
from jax import lax
from jax.experimental import pallas as pl
from jax.experimental.pallas import tpu as pltpu
from jax.sharding import PartitionSpec as P

MESH = pl.DeviceIdType.MESH
F32, BF16 = jnp.float32, jnp.bfloat16
WEIGHT = 0.5
OFFSET = 1e-05
RING = 4
CHUNKS = RING
ROWS = 16
BLOCK = 256
LANES = 128


def column_of(row):
    return jnp.broadcast_to(row, (LANES, LANES)).T


def kernel(
    copies, shards, hidden_in, gain_in, w_in, targets_in, partner_in, gg_out, tl_out,
    w, turned_w, hid, gain, targets, partner, xhat, normed, logits, dlog, stat_col, t_col, loss_col, turned, gacc,
    sx_src, sx_buf, sz_src, sz_buf, qs_row, cq_src, cq_line, cq_plane, fin_src, fin_buf,
    stage1, buf1_0, buf1_1, buf1_2, buf1_3, stage2, buf2,
    in_sem, z_send, z_recv, x_send, x_recv, sx_send, sx_recv, sz_send, sz_recv, cl_send, cl_recv, cp_send, cp_recv, f_send, f_recv,
    p1_send, p1_recv, p2_send, p2_recv,
):
    buf1 = (buf1_0, buf1_1, buf1_2, buf1_3)
    me_c, me_f = lax.axis_index("copy"), lax.axis_index("fsdp")
    me_x, me_z = me_f // RING, lax.rem(me_f, RING)
    line, plane = cq_line.shape[0], cq_plane.shape[0]
    depth, vocab = w.shape
    share = hid.shape[1]
    half_share = share // 2
    tokens = share * RING
    piece_rows, piece_cols = stage1.shape[2], stage1.shape[3]
    splits = vocab // piece_cols

    loads = [
        pltpu.make_async_copy(source, target, in_sem.at[i])
        for i, (source, target) in enumerate(
            ((hidden_in, hid.at[me_f]), (partner_in, partner), (targets_in, targets), (gain_in, gain), (w_in, w))
        )
    ]
    for load in loads:
        load.start()

    barrier = pltpu.get_barrier_semaphore()

    def greet_copy(k, carry):
        pl.semaphore_signal(barrier, inc=1, device_id=(lax.rem(me_c + k, copies), me_f), device_id_type=MESH)
        return carry

    def greet_shard(k, carry):
        pl.semaphore_signal(barrier, inc=1, device_id=(me_c, lax.rem(me_f + k, shards)), device_id_type=MESH)
        return carry

    lax.fori_loop(1, shards, greet_shard, 0)
    lax.fori_loop(1, copies, greet_copy, 0)
    pl.semaphore_wait(barrier, copies + shards - 2)
    loads[0].wait()

    def shard_of(dx, dz):
        return lax.rem(me_x + dx + RING, RING) * RING + lax.rem(me_z + dz + RING, RING)

    def hop(which, half, to, send, recv):
        rows = pl.ds(half * half_share, half_share)
        return pltpu.make_async_remote_copy(
            src_ref=hid.at[which, rows], dst_ref=hid.at[which, rows], send_sem=send, recv_sem=recv,
            device_id=(me_c, to), device_id_type=MESH,
        )

    def z_copy(half, slot):
        onward = 1 - 2 * half
        dz, to = ((0, onward), (0, -onward), (-onward, onward))[slot]
        at = half * 3 + slot
        return hop(shard_of(0, dz), half, shard_of(0, to), z_send.at[at], z_recv.at[at])

    CHUNK_Z = (0, -1, 1, 2)

    def x_copy(half, chunk, slot):
        onward = 1 - 2 * half
        dx, to = ((0, onward), (0, -onward), (-onward, onward))[slot]
        at = (half * CHUNKS + chunk) * 3 + slot
        return hop(shard_of(dx, CHUNK_Z[chunk]), half, shard_of(to, 0), x_send.at[at], x_recv.at[at])

    def spread(half, chunk):
        x_copy(half, chunk, 0).start()
        x_copy(half, chunk, 1).start()

    def pass_on(chunk):
        for half in (0, 1):
            x_copy(half, chunk, 0).wait_recv()
            x_copy(half, chunk, 2).start()

    def gather_end(chunk):
        for half in (0, 1):
            x_copy(half, chunk, 1).wait_recv()
            x_copy(half, chunk, 2).wait_recv()

    def place_of(copy):
        return copy // (2 * line) * 2 + lax.rem(copy, 2), lax.rem(copy // 2, line)

    def copy_at(spot, z):
        return spot // 2 * (2 * line) + z * 2 + lax.rem(spot, 2)

    mine = place_of(me_c)

    def to_all(axis, src_of, buf, send, recv):
        size = buf.shape[0]

        def step(k, carry):
            if axis == "copy":
                peer = lax.rem(me_c + k, size)
                device = (peer, me_f)
            elif axis == "fsdp":
                peer = lax.rem(me_f + k, size)
                device = (me_c, peer)
            elif axis == "line":
                peer = copy_at(mine[0], lax.rem(mine[1] + k, line))
                device = (peer, me_f)
            elif axis == "plane":
                peer = copy_at(lax.rem(mine[0] + k, plane), mine[1])
                device = (peer, me_f)
            elif axis == "x":
                peer = shard_of(k, 0)
                device = (me_c, peer)
            else:
                peer = shard_of(0, k)
                device = (me_c, peer)
            pltpu.make_async_remote_copy(
                src_ref=src_of(peer, k), dst_ref=buf.at[k], send_sem=send, recv_sem=recv,
                device_id=device, device_id_type=MESH,
            ).start()
            return carry

        lax.fori_loop(1, size, step, 0)

    def wait_all(buf, sem):
        if buf.shape[0] > 1:
            rest = buf.at[pl.ds(1, buf.shape[0] - 1)]
            pltpu.make_async_copy(rest, rest, sem).wait()

    def chunk_z(chunk):
        return lax.rem(me_z + CHUNK_Z[chunk] + RING, RING)

    def rows_of(chunk, g):
        return pl.ds(pl.multiple_of(chunk * tokens + g * ROWS, ROWS), ROWS)

    def rows(chunk, count=1):
        return slice(chunk * tokens, (chunk + count) * tokens)

    def lanes_of(part, chunk):
        return pl.ds(pl.multiple_of(part * wide + chunk_z(chunk) * LANES, LANES), LANES)

    def place(g):
        first = (g * ROWS) // piece_rows * splits
        return first, pl.ds(pl.multiple_of(lax.rem(g * ROWS, piece_rows), ROWS), ROWS)

    groups = tokens // ROWS
    wide = CHUNKS * LANES
    lane = lax.broadcasted_iota(jnp.int32, (ROWS, LANES), 1)

    def forward(chunk):
        z = chunk_z(chunk)

        def normalise(g, carry):
            at = rows_of(chunk, g)
            inside = pl.ds(pl.multiple_of(lax.rem(g * ROWS, share), ROWS), ROWS)
            value = hid[(g * ROWS) // share * RING + z, inside, :].astype(F32)
            scale = lax.rsqrt(jnp.mean(value * value, axis=-1, keepdims=True) + OFFSET)
            unit = value * scale
            xhat[at, :] = unit
            normed[at, :] = (unit * gain[...]).astype(BF16)
            return carry

        lax.fori_loop(0, groups, normalise, 0, unroll=2)

        def product(b, carry):
            cols = pl.ds(pl.multiple_of(b * BLOCK, BLOCK), BLOCK)
            logits[rows(chunk), cols] = jnp.dot(normed[rows(chunk), :], w[:, cols], preferred_element_type=F32)
            return carry

        lax.fori_loop(0, vocab // BLOCK, product, 0)

        def rounded(g, carry):
            at = rows_of(chunk, g)
            value = logits[at, :]
            top = jnp.max(value, axis=-1, keepdims=True)
            stat_col[at, :] = jnp.broadcast_to(top, (ROWS, LANES))
            short = (value - top).astype(BF16)
            first, inner = place(g)
            for split in range(splits):
                stage1[chunk, first + split, inner, :] = short[:, split * piece_cols : (split + 1) * piece_cols]
            return carry

        lax.fori_loop(0, groups, rounded, 0, unroll=2)

    def exchange_first(chunk):
        to_all("copy", lambda peer, k: stage1.at[chunk, peer], buf1[chunk], p1_send.at[chunk], p1_recv.at[chunk])
        buf1[chunk][0] = stage1[chunk, me_c]

    def sums(chunk):
        def step(g, carry):
            at = rows_of(chunk, g)
            top = stat_col[at, :]
            total = jnp.sum(jnp.exp(logits[at, :] - top[:, 0:1]), axis=-1, keepdims=True)
            first, inner = place(g)
            q_total = jnp.zeros((ROWS, 1), F32)
            for split in range(splits):
                short = stage1[chunk, first + split, inner, :].astype(F32)
                q_total = q_total + jnp.sum(jnp.exp(short), axis=-1, keepdims=True)
            stat_col[at, :] = jnp.where(lane == 0, top, jnp.where(lane == 1, total, q_total))
            return carry

        lax.fori_loop(0, groups, step, 0, unroll=2)
        flat = stat_col[rows(chunk), :].T
        for i in range(3):
            sx_src[:, lanes_of(i, chunk)] = flat[i : i + 1, :]

    def exchange_second(chunk):
        wait_all(buf1[chunk], p1_recv.at[chunk])

        def pick(j, carry):
            source = partner[lax.rem(me_c + j, copies)]
            stage2[chunk, j] = buf1[chunk][lax.rem(me_c - source + copies, copies)]
            return carry

        lax.fori_loop(0, copies, pick, 0)
        to_all("copy", lambda peer, k: stage2.at[chunk, k], buf2.at[chunk], p2_send.at[chunk], p2_recv.at[chunk])
        buf2[chunk, 0] = stage2[chunk, 0]

    def joined(parts):
        tops = parts[:, :, 0:wide]
        top = jnp.max(tops, axis=0)
        factor = jnp.exp(tops - top[None])
        total = jnp.sum(parts[:, :, wide : 2 * wide] * factor, axis=0)
        q_total = jnp.sum(parts[:, :, 2 * wide : 3 * wide] * factor, axis=0)
        return top, total, q_total

    def statistics_x():
        sx_buf[0] = sx_src[...]
        to_all("x", lambda peer, k: sx_src, sx_buf, sx_send.at[0], sx_recv.at[0])

    def statistics_z():
        wait_all(sx_buf, sx_recv.at[0])
        for i, value in enumerate(joined(sx_buf[...])):
            sz_src[:, i * wide : (i + 1) * wide] = value
        sz_buf[0] = sz_src[...]
        to_all("z", lambda peer, k: sz_src, sz_buf, sz_send.at[0], sz_recv.at[0])

    def statistics_copy():
        wait_all(sz_buf, sz_recv.at[0])
        top, total, q_total = joined(sz_buf[...])
        log_total = jnp.log(total)
        cq_src[:, 0:wide] = (sx_src[:, 0:wide] - top) - log_total
        cq_src[:, wide : 2 * wide] = q_total / total
        cq_line[0] = cq_src[...]
        to_all("line", lambda peer, k: cq_src, cq_line, cl_send.at[0], cl_recv.at[0])
        wait_all(sz_buf, sz_send.at[0])
        sz_src[:, 0:wide] = top
        sz_src[:, wide : 2 * wide] = log_total

    def statistics_plane():
        wait_all(cq_line, cl_recv.at[0])
        cq_plane[0] = cq_line[...]
        to_all("plane", lambda peer, k: cq_line, cq_plane, cp_send.at[0], cp_recv.at[0])

    def statistics_end():
        wait_all(cq_plane, cp_recv.at[0])
        spot, z = place_of(partner[me_c])
        qs_row[...] = cq_plane[lax.rem(mine[0] - spot + plane, plane), lax.rem(mine[1] - z + line, line)]
        for chunk in range(CHUNKS):
            turned[0:1, :] = sz_src[:, lanes_of(0, chunk)]
            turned[1:2, :] = sz_src[:, lanes_of(1, chunk)]
            turned[2:3, :] = qs_row[:, lanes_of(0, chunk)]
            turned[3:4, :] = qs_row[:, lanes_of(1, chunk)]
            stat_col[rows(chunk), :] = turned[...].T

    def slopes(chunk):
        wait_all(buf2.at[chunk], p2_recv.at[chunk])
        z = chunk_z(chunk)
        base = me_f * vocab

        def step(g, carry):
            at = rows_of(chunk, g)
            token = pl.ds(
                pl.multiple_of((g * ROWS) // share * tokens + z * share + lax.rem(g * ROWS, share), ROWS), ROWS
            )
            first, inner = place(g)
            top, log_total = stat_col[at, 0:1], stat_col[at, 1:2]
            lack, q_total = stat_col[at, 2:3], stat_col[at, 3:4]
            target = t_col[token, 0:1]
            loss = jnp.zeros((ROWS, 1), F32)
            for split in range(splits):
                cols = slice(split * piece_cols, (split + 1) * piece_cols)
                slot = lax.rem(me_c - (first + split) + copies, copies)
                logq = buf2[chunk, slot, inner, :].astype(F32) + lack
                q = jnp.exp(logq)
                value = (logits[at, cols] - top) - log_total
                prob = jnp.exp(value)
                ids = base + split * piece_cols + lax.broadcasted_iota(jnp.int32, (ROWS, piece_cols), 1)
                hot = ids == target
                term = WEIGHT * (q * (logq - value)) - jnp.where(hot, value, 0.0)
                loss = loss + jnp.sum(term, axis=-1, keepdims=True)
                slope = prob - jnp.where(hot, 1.0, 0.0) + WEIGHT * (q_total * prob - q)
                dlog[at, cols] = slope.astype(BF16)
            loss_col[token, :] = jnp.broadcast_to(loss, (ROWS, LANES))
            return carry

        lax.fori_loop(0, groups, step, 0, unroll=2)

    def turn_weights():
        def step(b, carry):
            at = pl.ds(pl.multiple_of(b * BLOCK, BLOCK), BLOCK)
            turned_w[:, at] = w[at, :].T
            return carry

        lax.fori_loop(0, depth // BLOCK, step, 0)

    def gradient(chunk, count):
        def product(b, carry):
            at = pl.ds(pl.multiple_of(b * BLOCK, BLOCK), BLOCK)
            piece = jnp.dot(dlog[rows(chunk, count), :], turned_w[:, at], preferred_element_type=F32)
            part = jnp.sum(xhat[rows(chunk, count), at] * piece, axis=0, keepdims=True)
            if chunk == 0:
                gacc[:, at] = part
            else:
                gacc[:, at] = gacc[:, at] + part
            return carry

        lax.fori_loop(0, depth // BLOCK, product, 0)

    def prepare():
        fin_src[...] = jnp.zeros_like(fin_src)
        turned[...] = jnp.zeros_like(turned)
        loads[2].wait()
        for part in range(CHUNKS * tokens // LANES):
            t_col[part * LANES : (part + 1) * LANES, :] = column_of(targets[part : part + 1, :])

    spread(0, 0)
    spread(1, 0)
    z_copy(0, 0).start()
    z_copy(1, 0).start()
    z_copy(0, 1).start()
    z_copy(1, 1).start()
    prepare()
    loads[1].wait()
    loads[3].wait()
    pass_on(0)
    loads[4].wait()
    turn_weights()
    gather_end(0)
    forward(0)
    exchange_first(0)
    z_copy(0, 0).wait_recv()
    z_copy(0, 2).start()
    spread(0, 1)
    z_copy(1, 0).wait_recv()
    z_copy(1, 2).start()
    spread(1, 2)
    sums(0)
    z_copy(1, 1).wait_recv()
    spread(1, 1)
    z_copy(0, 1).wait_recv()
    spread(0, 2)
    pass_on(1)
    pass_on(2)
    gather_end(1)
    forward(1)
    exchange_first(1)
    z_copy(0, 2).wait_recv()
    spread(0, 3)
    z_copy(1, 2).wait_recv()
    spread(1, 3)
    gather_end(2)
    forward(2)
    pass_on(3)
    exchange_first(2)
    sums(1)
    sums(2)
    exchange_second(0)
    gather_end(3)
    forward(3)
    sums(3)
    statistics_x()
    statistics_z()
    exchange_first(3)
    statistics_copy()
    exchange_second(1)
    statistics_plane()
    exchange_second(2)
    exchange_second(3)
    statistics_end()
    slopes(0)
    slopes(1)
    gradient(0, 2)
    slopes(2)
    slopes(3)
    gradient(2, 2)

    per_row = LANES // share
    for part in range(shards // per_row):
        row = loss_col[part * LANES : (part + 1) * LANES, :].T[0:1, :]
        for j in range(part * per_row, (part + 1) * per_row):
            fin_src[j, :, 0:LANES] = gacc[:, j * LANES : (j + 1) * LANES]
            fin_src[j, :, LANES : 2 * LANES] = row
    to_all("fsdp", lambda peer, k: fin_src.at[peer], fin_buf, f_send.at[0], f_recv.at[0])
    fin_buf[0] = fin_src[me_f]

    for half in (0, 1):
        for slot in range(3):
            z_copy(half, slot).wait_send()
            for chunk in range(CHUNKS):
                x_copy(half, chunk, slot).wait_send()
    for chunk in range(CHUNKS):
        wait_all(buf1[chunk], p1_send.at[chunk])
        wait_all(buf2.at[chunk], p2_send.at[chunk])
    wait_all(sx_buf, sx_send.at[0])
    wait_all(cq_line, cl_send.at[0])
    wait_all(cq_plane, cp_send.at[0])
    wait_all(fin_buf, f_send.at[0])

    wait_all(fin_buf, f_recv.at[0])
    whole = jnp.sum(fin_buf[...], axis=0)
    gg_out[...] = whole[:, 0:LANES]
    row = whole[:, LANES : 2 * LANES]
    result = row[:, 0:share]
    for k in range(1, per_row):
        result = jnp.where(lax.rem(me_f, per_row) == k, row[:, k * share : (k + 1) * share], result)
    tl_out[...] = result


def per_device(copies, shards, hidden, gain, head_weight, targets, partner):
    share, depth = hidden.shape[1], hidden.shape[2]
    vocab = head_weight.shape[2]
    tokens = share * shards
    chunk = share * RING
    groups = min(chunk // ROWS, copies)
    piece = (chunk // groups, vocab // (copies // groups))
    line = max(1, copies // 8)
    anywhere, vmem = pl.BlockSpec(memory_space=pl.ANY), pl.BlockSpec(memory_space=pltpu.VMEM)
    dma = pltpu.SemaphoreType.DMA
    return pl.pallas_call(
        functools.partial(kernel, copies, shards),
        out_shape=(
            jax.ShapeDtypeStruct((1, depth // shards), F32),
            jax.ShapeDtypeStruct((1, share), F32),
        ),
        in_specs=[anywhere] * 5,
        out_specs=(vmem, vmem),
        scratch_shapes=[
            pltpu.VMEM((depth, vocab), BF16),
            pltpu.VMEM((vocab, depth), BF16),
            pltpu.VMEM((shards, share, depth), BF16),
            pltpu.VMEM((1, depth), F32),
            pltpu.VMEM((tokens // LANES, LANES), jnp.int32),
            pltpu.SMEM((copies,), jnp.int32),
            pltpu.VMEM((tokens, depth), F32),
            pltpu.VMEM((tokens, depth), BF16),
            pltpu.VMEM((tokens, vocab), F32),
            pltpu.VMEM((tokens, vocab), BF16),
            pltpu.VMEM((tokens, LANES), F32),
            pltpu.VMEM((tokens, LANES), jnp.int32),
            pltpu.VMEM((tokens, LANES), F32),
            pltpu.VMEM((LANES, LANES), F32),
            pltpu.VMEM((1, depth), F32),
            pltpu.VMEM((1, 3 * tokens), F32),
            pltpu.VMEM((RING, 1, 3 * tokens), F32),
            pltpu.VMEM((1, 3 * tokens), F32),
            pltpu.VMEM((RING, 1, 3 * tokens), F32),
            pltpu.VMEM((1, 2 * tokens), F32),
            pltpu.VMEM((1, 2 * tokens), F32),
            pltpu.VMEM((line, 1, 2 * tokens), F32),
            pltpu.VMEM((copies // line, line, 1, 2 * tokens), F32),
            pltpu.VMEM((shards, 1, 2 * LANES), F32),
            pltpu.VMEM((shards, 1, 2 * LANES), F32),
            pltpu.VMEM((CHUNKS, copies) + piece, BF16),
        ]
        + [pltpu.VMEM((copies,) + piece, BF16)] * CHUNKS
        + [pltpu.VMEM((CHUNKS, copies) + piece, BF16)] * 2
        + [
            dma((5,)),
            dma((2 * 3,)),
            dma((2 * 3,)),
            dma((2 * CHUNKS * 3,)),
            dma((2 * CHUNKS * 3,)),
        ]
        + [dma((1,))] * 10
        + [dma((CHUNKS,))] * 4,
        compiler_params=pltpu.CompilerParams(
            collective_id=0, has_side_effects=True, vmem_limit_bytes=56 * 1024 * 1024
        ),
        cost_estimate=pl.CostEstimate(
            flops=4 * tokens * depth * vocab,
            bytes_accessed=2 * depth * vocab,
            transcendentals=4 * tokens * vocab,
        ),
    )(hidden[0], gain, head_weight[0], targets.reshape(-1, LANES), partner)


def solution(mesh):
    in_specs = (P("copy", "fsdp", None), P("copy", None), P("copy", None, "fsdp"), P(), P())
    out_specs = (P("copy", "fsdp"), P("copy", "fsdp"))
    return jax.shard_map(
        functools.partial(per_device, mesh.shape["copy"], mesh.shape["fsdp"]),
        mesh=mesh, in_specs=in_specs, out_specs=out_specs, check_vma=False,
    )
```

```python
import functools

import jax
import jax.numpy as jnp
from jax import lax
from jax.experimental import pallas as pl
from jax.experimental.pallas import tpu as pltpu
from jax.sharding import PartitionSpec as P

MESH = pl.DeviceIdType.MESH
F32, BF16 = jnp.float32, jnp.bfloat16
WEIGHT = 0.5
OFFSET = 1e-05
RING = 4
CHUNKS = RING
ROWS = 16
BLOCK = 256
LANES = 128


def column_of(row):
    return jnp.broadcast_to(row, (LANES, LANES)).T


def kernel(
    copies, shards, hidden_in, gain_in, w_in, targets_in, partner_in, gg_out, tl_out,
    w, turned_w, hid, gain, targets, partner, xhat, normed, logits, dlog, stat_col, t_col, loss_col, turned, gacc,
    sx_src, sx_buf, sz_src, sz_buf, qs_row, cq_src, cq_line, cq_plane, fin_src, fin_buf,
    stage1, buf1_0, buf1_1, buf1_2, buf1_3, stage2, buf2,
    in_sem, z_send, z_recv, x_send, x_recv, sx_send, sx_recv, sz_send, sz_recv, cl_send, cl_recv, cp_send, cp_recv, f_send, f_recv,
    p1_send, p1_recv, p2_send, p2_recv,
):
    buf1 = (buf1_0, buf1_1, buf1_2, buf1_3)
    me_c, me_f = lax.axis_index("copy"), lax.axis_index("fsdp")
    me_x, me_z = me_f // RING, lax.rem(me_f, RING)
    line, plane = cq_line.shape[0], cq_plane.shape[0]
    depth, vocab = w.shape
    share = hid.shape[1]
    half_share = share // 2
    tokens = share * RING
    piece_rows, piece_cols = stage1.shape[2], stage1.shape[3]
    splits = vocab // piece_cols

    loads = [
        pltpu.make_async_copy(source, target, in_sem.at[i])
        for i, (source, target) in enumerate(
            ((hidden_in, hid.at[me_f]), (partner_in, partner), (targets_in, targets), (gain_in, gain), (w_in, w))
        )
    ]
    for load in loads:
        load.start()

    def shard_of(dx, dz):
        return lax.rem(me_x + dx + RING, RING) * RING + lax.rem(me_z + dz + RING, RING)

    barrier = pltpu.get_barrier_semaphore()

    def greet_copy(k, carry):
        pl.semaphore_signal(barrier, inc=1, device_id=(lax.rem(me_c + k, copies), me_f), device_id_type=MESH)
        return carry

    for k in range(1, RING):
        for peer in (shard_of(k, 0), shard_of(0, k)):
            pl.semaphore_signal(barrier, inc=1, device_id=(me_c, peer), device_id_type=MESH)
    lax.fori_loop(1, copies, greet_copy, 0)
    pl.semaphore_wait(barrier, copies - 1 + 2 * (RING - 1))
    loads[0].wait()

    def hop(which, half, to, send, recv):
        rows = pl.ds(half * half_share, half_share)
        return pltpu.make_async_remote_copy(
            src_ref=hid.at[which, rows], dst_ref=hid.at[which, rows], send_sem=send, recv_sem=recv,
            device_id=(me_c, to), device_id_type=MESH,
        )

    def z_copy(half, slot):
        onward = 1 - 2 * half
        dz, to = ((0, onward), (0, -onward), (-onward, onward))[slot]
        at = half * 3 + slot
        return hop(shard_of(0, dz), half, shard_of(0, to), z_send.at[at], z_recv.at[at])

    CHUNK_Z = (0, -1, 1, 2)

    def x_copy(half, chunk, slot):
        onward = 1 - 2 * half
        dx, to = ((0, onward), (0, -onward), (-onward, onward))[slot]
        at = (half * CHUNKS + chunk) * 3 + slot
        return hop(shard_of(dx, CHUNK_Z[chunk]), half, shard_of(to, 0), x_send.at[at], x_recv.at[at])

    def spread(half, chunk):
        x_copy(half, chunk, 0).start()
        x_copy(half, chunk, 1).start()

    def pass_on(chunk):
        for half in (0, 1):
            x_copy(half, chunk, 0).wait_recv()
            x_copy(half, chunk, 2).start()

    def gather_end(chunk):
        for half in (0, 1):
            x_copy(half, chunk, 1).wait_recv()
            x_copy(half, chunk, 2).wait_recv()

    def place_of(copy):
        return copy // (2 * line) * 2 + lax.rem(copy, 2), lax.rem(copy // 2, line)

    def copy_at(spot, z):
        return spot // 2 * (2 * line) + z * 2 + lax.rem(spot, 2)

    mine = place_of(me_c)

    def to_all(axis, src_of, buf, send, recv):
        size = buf.shape[0]

        def step(k, carry):
            if axis == "copy":
                peer = lax.rem(me_c + k, size)
                device = (peer, me_f)
            elif axis == "fsdp":
                peer = lax.rem(me_f + k, size)
                device = (me_c, peer)
            elif axis == "line":
                peer = copy_at(mine[0], lax.rem(mine[1] + k, line))
                device = (peer, me_f)
            elif axis == "plane":
                peer = copy_at(lax.rem(mine[0] + k, plane), mine[1])
                device = (peer, me_f)
            elif axis == "x":
                peer = shard_of(k, 0)
                device = (me_c, peer)
            else:
                peer = shard_of(0, k)
                device = (me_c, peer)
            pltpu.make_async_remote_copy(
                src_ref=src_of(peer, k), dst_ref=buf.at[k], send_sem=send, recv_sem=recv,
                device_id=device, device_id_type=MESH,
            ).start()
            return carry

        lax.fori_loop(1, size, step, 0)

    def wait_all(buf, sem):
        if buf.shape[0] > 1:
            rest = buf.at[pl.ds(1, buf.shape[0] - 1)]
            pltpu.make_async_copy(rest, rest, sem).wait()

    def chunk_z(chunk):
        return lax.rem(me_z + CHUNK_Z[chunk] + RING, RING)

    def rows_of(chunk, g):
        return pl.ds(pl.multiple_of(chunk * tokens + g * ROWS, ROWS), ROWS)

    def rows(chunk, count=1):
        return slice(chunk * tokens, (chunk + count) * tokens)

    def lanes_of(part, chunk):
        return pl.ds(pl.multiple_of(part * wide + chunk_z(chunk) * LANES, LANES), LANES)

    def place(g):
        first = (g * ROWS) // piece_rows * splits
        return first, pl.ds(pl.multiple_of(lax.rem(g * ROWS, piece_rows), ROWS), ROWS)

    groups = tokens // ROWS
    wide = CHUNKS * LANES
    lane = lax.broadcasted_iota(jnp.int32, (ROWS, LANES), 1)

    def forward(chunk):
        z = chunk_z(chunk)

        def normalise(g, carry):
            at = rows_of(chunk, g)
            inside = pl.ds(pl.multiple_of(lax.rem(g * ROWS, share), ROWS), ROWS)
            value = hid[(g * ROWS) // share * RING + z, inside, :].astype(F32)
            scale = lax.rsqrt(jnp.mean(value * value, axis=-1, keepdims=True) + OFFSET)
            unit = value * scale
            xhat[at, :] = unit
            normed[at, :] = (unit * gain[...]).astype(BF16)
            return carry

        lax.fori_loop(0, groups, normalise, 0, unroll=2)

        def product(b, carry):
            cols = pl.ds(pl.multiple_of(b * BLOCK, BLOCK), BLOCK)
            logits[rows(chunk), cols] = jnp.dot(normed[rows(chunk), :], w[:, cols], preferred_element_type=F32)
            return carry

        lax.fori_loop(0, vocab // BLOCK, product, 0)

        def rounded(g, carry):
            at = rows_of(chunk, g)
            value = logits[at, :]
            top = jnp.max(value, axis=-1, keepdims=True)
            stat_col[at, :] = jnp.broadcast_to(top, (ROWS, LANES))
            short = (value - top).astype(BF16)
            first, inner = place(g)
            for split in range(splits):
                stage1[chunk, first + split, inner, :] = short[:, split * piece_cols : (split + 1) * piece_cols]
            return carry

        lax.fori_loop(0, groups, rounded, 0, unroll=2)

    def exchange_first(chunk):
        to_all("copy", lambda peer, k: stage1.at[chunk, peer], buf1[chunk], p1_send.at[chunk], p1_recv.at[chunk])
        buf1[chunk][0] = stage1[chunk, me_c]

    def sums(chunk):
        def step(g, carry):
            at = rows_of(chunk, g)
            top = stat_col[at, :]
            total = jnp.sum(jnp.exp(logits[at, :] - top[:, 0:1]), axis=-1, keepdims=True)
            first, inner = place(g)
            q_total = jnp.zeros((ROWS, 1), F32)
            for split in range(splits):
                short = stage1[chunk, first + split, inner, :].astype(F32)
                q_total = q_total + jnp.sum(jnp.exp(short), axis=-1, keepdims=True)
            stat_col[at, :] = jnp.where(lane == 0, top, jnp.where(lane == 1, total, q_total))
            return carry

        lax.fori_loop(0, groups, step, 0, unroll=2)
        flat = stat_col[rows(chunk), :].T
        for i in range(3):
            sx_src[:, lanes_of(i, chunk)] = flat[i : i + 1, :]

    def exchange_second(chunk):
        wait_all(buf1[chunk], p1_recv.at[chunk])

        def pick(j, carry):
            source = partner[lax.rem(me_c + j, copies)]
            stage2[chunk, j] = buf1[chunk][lax.rem(me_c - source + copies, copies)]
            return carry

        lax.fori_loop(0, copies, pick, 0)
        to_all("copy", lambda peer, k: stage2.at[chunk, k], buf2.at[chunk], p2_send.at[chunk], p2_recv.at[chunk])
        buf2[chunk, 0] = stage2[chunk, 0]

    def joined(parts):
        tops = parts[:, :, 0:wide]
        top = jnp.max(tops, axis=0)
        factor = jnp.exp(tops - top[None])
        total = jnp.sum(parts[:, :, wide : 2 * wide] * factor, axis=0)
        q_total = jnp.sum(parts[:, :, 2 * wide : 3 * wide] * factor, axis=0)
        return top, total, q_total

    def statistics_x():
        sx_buf[0] = sx_src[...]
        to_all("x", lambda peer, k: sx_src, sx_buf, sx_send.at[0], sx_recv.at[0])

    def statistics_z():
        wait_all(sx_buf, sx_recv.at[0])
        for i, value in enumerate(joined(sx_buf[...])):
            sz_src[:, i * wide : (i + 1) * wide] = value
        sz_buf[0] = sz_src[...]
        to_all("z", lambda peer, k: sz_src, sz_buf, sz_send.at[0], sz_recv.at[0])

    def statistics_copy():
        wait_all(sz_buf, sz_recv.at[0])
        top, total, q_total = joined(sz_buf[...])
        log_total = jnp.log(total)
        cq_src[:, 0:wide] = (sx_src[:, 0:wide] - top) - log_total
        cq_src[:, wide : 2 * wide] = q_total / total
        cq_line[0] = cq_src[...]
        to_all("line", lambda peer, k: cq_src, cq_line, cl_send.at[0], cl_recv.at[0])
        wait_all(sz_buf, sz_send.at[0])
        sz_src[:, 0:wide] = top
        sz_src[:, wide : 2 * wide] = log_total

    def statistics_plane():
        wait_all(cq_line, cl_recv.at[0])
        cq_plane[0] = cq_line[...]
        to_all("plane", lambda peer, k: cq_line, cq_plane, cp_send.at[0], cp_recv.at[0])

    def statistics_end():
        wait_all(cq_plane, cp_recv.at[0])
        spot, z = place_of(partner[me_c])
        qs_row[...] = cq_plane[lax.rem(mine[0] - spot + plane, plane), lax.rem(mine[1] - z + line, line)]
        for chunk in range(CHUNKS):
            turned[0:1, :] = sz_src[:, lanes_of(0, chunk)]
            turned[1:2, :] = sz_src[:, lanes_of(1, chunk)]
            turned[2:3, :] = qs_row[:, lanes_of(0, chunk)]
            turned[3:4, :] = qs_row[:, lanes_of(1, chunk)]
            stat_col[rows(chunk), :] = turned[...].T

    def slopes(chunk):
        wait_all(buf2.at[chunk], p2_recv.at[chunk])
        z = chunk_z(chunk)
        base = me_f * vocab

        def step(g, carry):
            at = rows_of(chunk, g)
            token = pl.ds(
                pl.multiple_of((g * ROWS) // share * tokens + z * share + lax.rem(g * ROWS, share), ROWS), ROWS
            )
            first, inner = place(g)
            top, log_total = stat_col[at, 0:1], stat_col[at, 1:2]
            lack, q_total = stat_col[at, 2:3], stat_col[at, 3:4]
            target = t_col[token, 0:1]
            loss = jnp.zeros((ROWS, 1), F32)
            for split in range(splits):
                cols = slice(split * piece_cols, (split + 1) * piece_cols)
                slot = lax.rem(me_c - (first + split) + copies, copies)
                logq = buf2[chunk, slot, inner, :].astype(F32) + lack
                q = jnp.exp(logq)
                value = (logits[at, cols] - top) - log_total
                prob = jnp.exp(value)
                ids = base + split * piece_cols + lax.broadcasted_iota(jnp.int32, (ROWS, piece_cols), 1)
                hot = ids == target
                term = WEIGHT * (q * (logq - value)) - jnp.where(hot, value, 0.0)
                loss = loss + jnp.sum(term, axis=-1, keepdims=True)
                slope = prob - jnp.where(hot, 1.0, 0.0) + WEIGHT * (q_total * prob - q)
                dlog[at, cols] = slope.astype(BF16)
            loss_col[at, :] = jnp.broadcast_to(loss, (ROWS, LANES))
            return carry

        lax.fori_loop(0, groups, step, 0, unroll=2)

    def turn_weights():
        def step(b, carry):
            at = pl.ds(pl.multiple_of(b * BLOCK, BLOCK), BLOCK)
            turned_w[:, at] = w[at, :].T
            return carry

        lax.fori_loop(0, depth // BLOCK, step, 0)

    def losses(chunk):
        row = loss_col[rows(chunk), :].T[0:1, :]
        for x in range(RING):
            fin_src[x * RING + chunk_z(chunk), :, LANES : 2 * LANES] = row

    def gradient(chunk, count):
        def product(b, carry):
            at = pl.ds(pl.multiple_of(b * BLOCK, BLOCK), BLOCK)
            piece = jnp.dot(dlog[rows(chunk, count), :], turned_w[:, at], preferred_element_type=F32)
            part = jnp.sum(xhat[rows(chunk, count), at] * piece, axis=0, keepdims=True)
            if chunk == 0:
                gacc[:, at] = part
            else:
                gacc[:, at] = gacc[:, at] + part
            return carry

        lax.fori_loop(0, depth // BLOCK, product, 0)

    def prepare():
        fin_src[...] = jnp.zeros_like(fin_src)
        turned[...] = jnp.zeros_like(turned)
        loads[2].wait()
        for part in range(CHUNKS * tokens // LANES):
            t_col[part * LANES : (part + 1) * LANES, :] = column_of(targets[part : part + 1, :])

    spread(0, 0)
    spread(1, 0)
    z_copy(0, 0).start()
    z_copy(1, 0).start()
    z_copy(0, 1).start()
    z_copy(1, 1).start()
    prepare()
    loads[1].wait()
    loads[3].wait()
    pass_on(0)
    loads[4].wait()
    turn_weights()
    gather_end(0)
    forward(0)
    exchange_first(0)
    z_copy(0, 0).wait_recv()
    z_copy(0, 2).start()
    spread(0, 1)
    z_copy(1, 0).wait_recv()
    z_copy(1, 2).start()
    spread(1, 2)
    sums(0)
    z_copy(1, 1).wait_recv()
    spread(1, 1)
    z_copy(0, 1).wait_recv()
    spread(0, 2)
    pass_on(1)
    pass_on(2)
    gather_end(1)
    forward(1)
    exchange_first(1)
    z_copy(0, 2).wait_recv()
    spread(0, 3)
    z_copy(1, 2).wait_recv()
    spread(1, 3)
    gather_end(2)
    forward(2)
    pass_on(3)
    exchange_first(2)
    sums(1)
    sums(2)
    exchange_second(0)
    gather_end(3)
    forward(3)
    sums(3)
    statistics_x()
    statistics_z()
    exchange_first(3)
    statistics_copy()
    exchange_second(1)
    statistics_plane()
    exchange_second(2)
    exchange_second(3)
    statistics_end()
    slopes(0)
    slopes(1)
    gradient(0, 2)
    losses(0)
    losses(1)
    slopes(2)
    slopes(3)
    gradient(2, 2)

    for j in range(shards):
        fin_src[j, :, 0:LANES] = gacc[:, j * LANES : (j + 1) * LANES]
    losses(2)
    losses(3)
    to_all("fsdp", lambda peer, k: fin_src.at[peer], fin_buf, f_send.at[0], f_recv.at[0])
    fin_buf[0] = fin_src[me_f]

    for half in (0, 1):
        for slot in range(3):
            z_copy(half, slot).wait_send()
            for chunk in range(CHUNKS):
                x_copy(half, chunk, slot).wait_send()
    for chunk in range(CHUNKS):
        wait_all(buf1[chunk], p1_send.at[chunk])
        wait_all(buf2.at[chunk], p2_send.at[chunk])
    wait_all(sx_buf, sx_send.at[0])
    wait_all(cq_line, cl_send.at[0])
    wait_all(cq_plane, cp_send.at[0])

    wait_all(fin_buf, f_send.at[0])
    wait_all(fin_buf, f_recv.at[0])
    whole = jnp.sum(fin_buf[...], axis=0)
    gg_out[...] = whole[:, 0:LANES]
    row = whole[:, LANES : 2 * LANES]
    result = row[:, 0:share]
    for k in range(1, RING):
        result = jnp.where(me_x == k, row[:, k * share : (k + 1) * share], result)
    tl_out[...] = result


def per_device(copies, shards, hidden, gain, head_weight, targets, partner):
    share, depth = hidden.shape[1], hidden.shape[2]
    vocab = head_weight.shape[2]
    tokens = share * shards
    chunk = share * RING
    groups = min(chunk // ROWS, copies)
    piece = (chunk // groups, vocab // (copies // groups))
    line = max(1, copies // 8)
    anywhere, vmem = pl.BlockSpec(memory_space=pl.ANY), pl.BlockSpec(memory_space=pltpu.VMEM)
    dma = pltpu.SemaphoreType.DMA
    return pl.pallas_call(
        functools.partial(kernel, copies, shards),
        out_shape=(
            jax.ShapeDtypeStruct((1, depth // shards), F32),
            jax.ShapeDtypeStruct((1, share), F32),
        ),
        in_specs=[anywhere] * 5,
        out_specs=(vmem, vmem),
        scratch_shapes=[
            pltpu.VMEM((depth, vocab), BF16),
            pltpu.VMEM((vocab, depth), BF16),
            pltpu.VMEM((shards, share, depth), BF16),
            pltpu.VMEM((1, depth), F32),
            pltpu.VMEM((tokens // LANES, LANES), jnp.int32),
            pltpu.SMEM((copies,), jnp.int32),
            pltpu.VMEM((tokens, depth), F32),
            pltpu.VMEM((tokens, depth), BF16),
            pltpu.VMEM((tokens, vocab), F32),
            pltpu.VMEM((tokens, vocab), BF16),
            pltpu.VMEM((tokens, LANES), F32),
            pltpu.VMEM((tokens, LANES), jnp.int32),
            pltpu.VMEM((tokens, LANES), F32),
            pltpu.VMEM((LANES, LANES), F32),
            pltpu.VMEM((1, depth), F32),
            pltpu.VMEM((1, 3 * tokens), F32),
            pltpu.VMEM((RING, 1, 3 * tokens), F32),
            pltpu.VMEM((1, 3 * tokens), F32),
            pltpu.VMEM((RING, 1, 3 * tokens), F32),
            pltpu.VMEM((1, 2 * tokens), F32),
            pltpu.VMEM((1, 2 * tokens), F32),
            pltpu.VMEM((line, 1, 2 * tokens), F32),
            pltpu.VMEM((copies // line, line, 1, 2 * tokens), F32),
            pltpu.VMEM((shards, 1, 2 * LANES), F32),
            pltpu.VMEM((shards, 1, 2 * LANES), F32),
            pltpu.VMEM((CHUNKS, copies) + piece, BF16),
        ]
        + [pltpu.VMEM((copies,) + piece, BF16)] * CHUNKS
        + [pltpu.VMEM((CHUNKS, copies) + piece, BF16)] * 2
        + [
            dma((5,)),
            dma((2 * 3,)),
            dma((2 * 3,)),
            dma((2 * CHUNKS * 3,)),
            dma((2 * CHUNKS * 3,)),
        ]
        + [dma((1,))] * 10
        + [dma((CHUNKS,))] * 4,
        compiler_params=pltpu.CompilerParams(
            collective_id=0, has_side_effects=True, vmem_limit_bytes=56 * 1024 * 1024
        ),
        cost_estimate=pl.CostEstimate(
            flops=4 * tokens * depth * vocab,
            bytes_accessed=2 * depth * vocab,
            transcendentals=4 * tokens * vocab,
        ),
    )(hidden[0], gain, head_weight[0], targets.reshape(-1, LANES), partner)


def solution(mesh):
    in_specs = (P("copy", "fsdp", None), P("copy", None), P("copy", None, "fsdp"), P(), P())
    out_specs = (P("copy", "fsdp"), P("copy", "fsdp"))
    return jax.shard_map(
        functools.partial(per_device, mesh.shape["copy"], mesh.shape["fsdp"]),
        mesh=mesh, in_specs=in_specs, out_specs=out_specs, check_vma=False,
    )
```

```python
import functools

import jax
import jax.numpy as jnp
from jax import lax
from jax.experimental import pallas as pl
from jax.experimental.pallas import tpu as pltpu
from jax.sharding import PartitionSpec as P

MESH = pl.DeviceIdType.MESH
F32, BF16 = jnp.float32, jnp.bfloat16
WEIGHT = 0.5
OFFSET = 1e-05
RING = 4
CHUNKS = RING
ROWS = 16
BLOCK = 256
LANES = 128


def column_of(row):
    return jnp.broadcast_to(row, (LANES, LANES)).T


def kernel(
    copies, shards, hidden_in, gain_in, w_in, targets_in, partner_in, gg_out, tl_out,
    w, turned_w, hid, gain, targets, partner, xhat, normed, logits, dlog, stat_col, t_col, loss_col, turned, gacc,
    sx_src, sx_buf, sz_src, sz_buf, qs_row, cq_src, cq_line, cq_plane, fin_src, fin_buf,
    stage1, buf1_0, buf1_1, buf1_2, buf1_3, stage2, buf2,
    line_sem, in_sem, z_send, z_recv, x_send, x_recv, sx_send, sx_recv, sz_send, sz_recv, cl_send, cl_recv, cp_send, cp_recv, f_send, f_recv,
    p1_send, p1_recv, p2_send, p2_recv,
):
    buf1 = (buf1_0, buf1_1, buf1_2, buf1_3)
    me_c, me_f = lax.axis_index("copy"), lax.axis_index("fsdp")
    me_x, me_z = me_f // RING, lax.rem(me_f, RING)
    line, plane = cq_line.shape[0], cq_plane.shape[0]
    depth, vocab = w.shape
    share = hid.shape[1]
    half_share = share // 2
    tokens = share * RING
    piece_rows, piece_cols = stage1.shape[2], stage1.shape[3]
    splits = vocab // piece_cols

    loads = [
        pltpu.make_async_copy(source, target, in_sem.at[i])
        for i, (source, target) in enumerate(
            ((hidden_in, hid.at[me_f]), (partner_in, partner), (targets_in, targets), (gain_in, gain), (w_in, w))
        )
    ]
    for load in loads:
        load.start()

    def shard_of(dx, dz):
        return lax.rem(me_x + dx + RING, RING) * RING + lax.rem(me_z + dz + RING, RING)

    def place_of(copy):
        return copy // (2 * line) * 2 + lax.rem(copy, 2), lax.rem(copy // 2, line)

    def copy_at(spot, z):
        return spot // 2 * (2 * line) + z * 2 + lax.rem(spot, 2)

    mine = place_of(me_c)

    barrier = pltpu.get_barrier_semaphore()

    for k in range(1, RING):
        for peer in (shard_of(k, 0), shard_of(0, k)):
            pl.semaphore_signal(barrier, inc=1, device_id=(me_c, peer), device_id_type=MESH)
    plane_peers = [copy_at(lax.rem(mine[0] + k, plane), mine[1]) for k in range(1, plane)]
    line_peers = [copy_at(mine[0], lax.rem(mine[1] + k, line)) for k in range(1, line)]
    for peer in line_peers + plane_peers:
        pl.semaphore_signal(barrier, inc=1, device_id=(peer, me_f), device_id_type=MESH)
    pl.semaphore_wait(barrier, line + plane - 2 + 2 * (RING - 1))
    loads[0].wait()

    def hop(which, half, to, send, recv):
        rows = pl.ds(half * half_share, half_share)
        return pltpu.make_async_remote_copy(
            src_ref=hid.at[which, rows], dst_ref=hid.at[which, rows], send_sem=send, recv_sem=recv,
            device_id=(me_c, to), device_id_type=MESH,
        )

    def z_copy(half, slot):
        onward = 1 - 2 * half
        dz, to = ((0, onward), (0, -onward), (-onward, onward))[slot]
        at = half * 3 + slot
        return hop(shard_of(0, dz), half, shard_of(0, to), z_send.at[at], z_recv.at[at])

    CHUNK_Z = (0, -1, 1, 2)

    def x_copy(half, chunk, slot):
        onward = 1 - 2 * half
        dx, to = ((0, onward), (0, -onward), (-onward, onward))[slot]
        at = (half * CHUNKS + chunk) * 3 + slot
        return hop(shard_of(dx, CHUNK_Z[chunk]), half, shard_of(to, 0), x_send.at[at], x_recv.at[at])

    def spread(half, chunk):
        x_copy(half, chunk, 0).start()
        x_copy(half, chunk, 1).start()

    def pass_on(chunk):
        for half in (0, 1):
            x_copy(half, chunk, 0).wait_recv()
            x_copy(half, chunk, 2).start()

    def gather_end(chunk):
        for half in (0, 1):
            x_copy(half, chunk, 1).wait_recv()
            x_copy(half, chunk, 2).wait_recv()

    def to_all(axis, src_of, buf, send, recv):
        size = buf.shape[0]

        def step(k, carry):
            if axis == "copy":
                peer = lax.rem(me_c + k, size)
                device = (peer, me_f)
            elif axis == "fsdp":
                peer = lax.rem(me_f + k, size)
                device = (me_c, peer)
            elif axis == "line":
                peer = copy_at(mine[0], lax.rem(mine[1] + k, line))
                device = (peer, me_f)
            elif axis == "plane":
                peer = copy_at(lax.rem(mine[0] + k, plane), mine[1])
                device = (peer, me_f)
            elif axis == "x":
                peer = shard_of(k, 0)
                device = (me_c, peer)
            else:
                peer = shard_of(0, k)
                device = (me_c, peer)
            pltpu.make_async_remote_copy(
                src_ref=src_of(peer, k), dst_ref=buf.at[k], send_sem=send, recv_sem=recv,
                device_id=device, device_id_type=MESH,
            ).start()
            return carry

        lax.fori_loop(1, size, step, 0)

    def wait_all(buf, sem):
        if buf.shape[0] > 1:
            rest = buf.at[pl.ds(1, buf.shape[0] - 1)]
            pltpu.make_async_copy(rest, rest, sem).wait()

    def chunk_z(chunk):
        return lax.rem(me_z + CHUNK_Z[chunk] + RING, RING)

    def rows_of(chunk, g):
        return pl.ds(pl.multiple_of(chunk * tokens + g * ROWS, ROWS), ROWS)

    def rows(chunk, count=1):
        return slice(chunk * tokens, (chunk + count) * tokens)

    def lanes_of(part, chunk):
        return pl.ds(pl.multiple_of(part * wide + chunk_z(chunk) * LANES, LANES), LANES)

    def place(g):
        first = (g * ROWS) // piece_rows * splits
        return first, pl.ds(pl.multiple_of(lax.rem(g * ROWS, piece_rows), ROWS), ROWS)

    groups = tokens // ROWS
    wide = CHUNKS * LANES
    lane = lax.broadcasted_iota(jnp.int32, (ROWS, LANES), 1)

    def forward(chunk):
        z = chunk_z(chunk)

        def normalise(g, carry):
            at = rows_of(chunk, g)
            inside = pl.ds(pl.multiple_of(lax.rem(g * ROWS, share), ROWS), ROWS)
            value = hid[(g * ROWS) // share * RING + z, inside, :].astype(F32)
            scale = lax.rsqrt(jnp.mean(value * value, axis=-1, keepdims=True) + OFFSET)
            unit = value * scale
            xhat[at, :] = unit
            normed[at, :] = (unit * gain[...]).astype(BF16)
            return carry

        lax.fori_loop(0, groups, normalise, 0, unroll=2)

        def product(b, carry):
            cols = pl.ds(pl.multiple_of(b * BLOCK, BLOCK), BLOCK)
            logits[rows(chunk), cols] = jnp.dot(normed[rows(chunk), :], w[:, cols], preferred_element_type=F32)
            return carry

        lax.fori_loop(0, vocab // BLOCK, product, 0)

        def rounded(g, carry):
            at = rows_of(chunk, g)
            value = logits[at, :]
            top = jnp.max(value, axis=-1, keepdims=True)
            stat_col[at, :] = jnp.broadcast_to(top, (ROWS, LANES))
            short = (value - top).astype(BF16)
            first, inner = place(g)
            for split in range(splits):
                stage1[chunk, first + split, inner, :] = short[:, split * piece_cols : (split + 1) * piece_cols]
            return carry

        lax.fori_loop(0, groups, rounded, 0, unroll=2)

    def exchange_first(chunk):
        to_all("copy", lambda peer, k: stage1.at[chunk, peer], buf1[chunk], p1_send.at[chunk], p1_recv.at[chunk])
        buf1[chunk][0] = stage1[chunk, me_c]

    def sums(chunk):
        def step(g, carry):
            at = rows_of(chunk, g)
            top = stat_col[at, :]
            total = jnp.sum(jnp.exp(logits[at, :] - top[:, 0:1]), axis=-1, keepdims=True)
            first, inner = place(g)
            q_total = jnp.zeros((ROWS, 1), F32)
            for split in range(splits):
                short = stage1[chunk, first + split, inner, :].astype(F32)
                q_total = q_total + jnp.sum(jnp.exp(short), axis=-1, keepdims=True)
            stat_col[at, :] = jnp.where(lane == 0, top, jnp.where(lane == 1, total, q_total))
            return carry

        lax.fori_loop(0, groups, step, 0, unroll=2)
        flat = stat_col[rows(chunk), :].T
        for i in range(3):
            sx_src[:, lanes_of(i, chunk)] = flat[i : i + 1, :]

    def exchange_second(chunk):
        wait_all(buf1[chunk], p1_recv.at[chunk])

        def pick(j, carry):
            source = partner[lax.rem(me_c + j, copies)]
            stage2[chunk, j] = buf1[chunk][lax.rem(me_c - source + copies, copies)]
            return carry

        lax.fori_loop(0, copies, pick, 0)
        to_all("copy", lambda peer, k: stage2.at[chunk, k], buf2.at[chunk], p2_send.at[chunk], p2_recv.at[chunk])
        buf2[chunk, 0] = stage2[chunk, 0]

    def joined(parts):
        tops = parts[:, :, 0:wide]
        top = jnp.max(tops, axis=0)
        factor = jnp.exp(tops - top[None])
        total = jnp.sum(parts[:, :, wide : 2 * wide] * factor, axis=0)
        q_total = jnp.sum(parts[:, :, 2 * wide : 3 * wide] * factor, axis=0)
        return top, total, q_total

    def statistics_x():
        sx_buf[0] = sx_src[...]
        to_all("x", lambda peer, k: sx_src, sx_buf, sx_send.at[0], sx_recv.at[0])

    def statistics_z():
        wait_all(sx_buf, sx_recv.at[0])
        for i, value in enumerate(joined(sx_buf[...])):
            sz_src[:, i * wide : (i + 1) * wide] = value
        sz_buf[0] = sz_src[...]
        to_all("z", lambda peer, k: sz_src, sz_buf, sz_send.at[0], sz_recv.at[0])

    def statistics_copy():
        wait_all(sz_buf, sz_recv.at[0])
        top, total, q_total = joined(sz_buf[...])
        log_total = jnp.log(total)
        cq_src[:, 0:wide] = (sx_src[:, 0:wide] - top) - log_total
        cq_src[:, wide : 2 * wide] = q_total / total
        cq_line[0] = cq_src[...]
        to_all("line", lambda peer, k: cq_src, cq_line, cl_send.at[0], cl_recv.at[0])
        wait_all(sz_buf, sz_send.at[0])
        sz_src[:, 0:wide] = top
        sz_src[:, wide : 2 * wide] = log_total

    def statistics_plane():
        wait_all(cq_line, cl_recv.at[0])
        cq_plane[0] = cq_line[...]
        to_all("plane", lambda peer, k: cq_line, cq_plane, cp_send.at[0], cp_recv.at[0])

    def statistics_end():
        wait_all(cq_plane, cp_recv.at[0])
        spot, z = place_of(partner[me_c])
        qs_row[...] = cq_plane[lax.rem(mine[0] - spot + plane, plane), lax.rem(mine[1] - z + line, line)]
        for chunk in range(CHUNKS):
            turned[0:1, :] = sz_src[:, lanes_of(0, chunk)]
            turned[1:2, :] = sz_src[:, lanes_of(1, chunk)]
            turned[2:3, :] = qs_row[:, lanes_of(0, chunk)]
            turned[3:4, :] = qs_row[:, lanes_of(1, chunk)]
            stat_col[rows(chunk), :] = turned[...].T

    def slopes(chunk):
        wait_all(buf2.at[chunk], p2_recv.at[chunk])
        z = chunk_z(chunk)
        base = me_f * vocab

        def step(g, carry):
            at = rows_of(chunk, g)
            token = pl.ds(
                pl.multiple_of((g * ROWS) // share * tokens + z * share + lax.rem(g * ROWS, share), ROWS), ROWS
            )
            first, inner = place(g)
            top, log_total = stat_col[at, 0:1], stat_col[at, 1:2]
            lack, q_total = stat_col[at, 2:3], stat_col[at, 3:4]
            target = t_col[token, 0:1]
            loss = jnp.zeros((ROWS, 1), F32)
            for split in range(splits):
                cols = slice(split * piece_cols, (split + 1) * piece_cols)
                slot = lax.rem(me_c - (first + split) + copies, copies)
                logq = buf2[chunk, slot, inner, :].astype(F32) + lack
                q = jnp.exp(logq)
                value = (logits[at, cols] - top) - log_total
                prob = jnp.exp(value)
                ids = base + split * piece_cols + lax.broadcasted_iota(jnp.int32, (ROWS, piece_cols), 1)
                hot = ids == target
                term = WEIGHT * (q * (logq - value)) - jnp.where(hot, value, 0.0)
                loss = loss + jnp.sum(term, axis=-1, keepdims=True)
                slope = prob - jnp.where(hot, 1.0, 0.0) + WEIGHT * (q_total * prob - q)
                dlog[at, cols] = slope.astype(BF16)
            loss_col[at, :] = jnp.broadcast_to(loss, (ROWS, LANES))
            return carry

        lax.fori_loop(0, groups, step, 0, unroll=2)

    def turn_weights():
        def step(b, carry):
            at = pl.ds(pl.multiple_of(b * BLOCK, BLOCK), BLOCK)
            turned_w[:, at] = w[at, :].T
            return carry

        lax.fori_loop(0, depth // BLOCK, step, 0)

    def losses(chunk):
        row = loss_col[rows(chunk), :].T[0:1, :]
        for x in range(RING):
            fin_src[x * RING + chunk_z(chunk), :, LANES : 2 * LANES] = row

    def gradient(chunk, count):
        def product(b, carry):
            at = pl.ds(pl.multiple_of(b * BLOCK, BLOCK), BLOCK)
            piece = jnp.dot(dlog[rows(chunk, count), :], turned_w[:, at], preferred_element_type=F32)
            part = jnp.sum(xhat[rows(chunk, count), at] * piece, axis=0, keepdims=True)
            if chunk == 0:
                gacc[:, at] = part
            else:
                gacc[:, at] = gacc[:, at] + part
            return carry

        lax.fori_loop(0, depth // BLOCK, product, 0)

    def prepare():
        fin_src[...] = jnp.zeros_like(fin_src)
        turned[...] = jnp.zeros_like(turned)
        loads[2].wait()
        for part in range(CHUNKS * tokens // LANES):
            t_col[part * LANES : (part + 1) * LANES, :] = column_of(targets[part : part + 1, :])

    spread(0, 0)
    spread(1, 0)
    z_copy(0, 0).start()
    z_copy(1, 0).start()
    z_copy(0, 1).start()
    z_copy(1, 1).start()
    for peer in plane_peers:
        pl.semaphore_signal(line_sem, inc=1, device_id=(peer, me_f), device_id_type=MESH)
    prepare()
    loads[1].wait()
    loads[3].wait()
    pass_on(0)
    loads[4].wait()
    turn_weights()
    gather_end(0)
    forward(0)
    pl.semaphore_wait(line_sem, plane - 1)
    exchange_first(0)
    z_copy(0, 0).wait_recv()
    z_copy(0, 2).start()
    spread(0, 1)
    z_copy(1, 0).wait_recv()
    z_copy(1, 2).start()
    spread(1, 2)
    sums(0)
    z_copy(1, 1).wait_recv()
    spread(1, 1)
    z_copy(0, 1).wait_recv()
    spread(0, 2)
    pass_on(1)
    pass_on(2)
    gather_end(1)
    forward(1)
    exchange_first(1)
    z_copy(0, 2).wait_recv()
    spread(0, 3)
    z_copy(1, 2).wait_recv()
    spread(1, 3)
    gather_end(2)
    forward(2)
    pass_on(3)
    exchange_first(2)
    sums(1)
    sums(2)
    exchange_second(0)
    gather_end(3)
    forward(3)
    sums(3)
    statistics_x()
    statistics_z()
    exchange_first(3)
    statistics_copy()
    exchange_second(1)
    statistics_plane()
    exchange_second(2)
    exchange_second(3)
    statistics_end()
    slopes(0)
    slopes(1)
    gradient(0, 2)
    losses(0)
    losses(1)
    slopes(2)
    slopes(3)
    gradient(2, 2)

    for j in range(shards):
        fin_src[j, :, 0:LANES] = gacc[:, j * LANES : (j + 1) * LANES]
    losses(2)
    losses(3)
    to_all("fsdp", lambda peer, k: fin_src.at[peer], fin_buf, f_send.at[0], f_recv.at[0])
    fin_buf[0] = fin_src[me_f]

    for half in (0, 1):
        for slot in range(3):
            z_copy(half, slot).wait_send()
            for chunk in range(CHUNKS):
                x_copy(half, chunk, slot).wait_send()
    for chunk in range(CHUNKS):
        wait_all(buf1[chunk], p1_send.at[chunk])
        wait_all(buf2.at[chunk], p2_send.at[chunk])
    wait_all(sx_buf, sx_send.at[0])
    wait_all(cq_line, cl_send.at[0])
    wait_all(cq_plane, cp_send.at[0])

    wait_all(fin_buf, f_send.at[0])
    wait_all(fin_buf, f_recv.at[0])
    whole = jnp.sum(fin_buf[...], axis=0)
    gg_out[...] = whole[:, 0:LANES]
    row = whole[:, LANES : 2 * LANES]
    result = row[:, 0:share]
    for k in range(1, RING):
        result = jnp.where(me_x == k, row[:, k * share : (k + 1) * share], result)
    tl_out[...] = result


def per_device(copies, shards, hidden, gain, head_weight, targets, partner):
    share, depth = hidden.shape[1], hidden.shape[2]
    vocab = head_weight.shape[2]
    tokens = share * shards
    chunk = share * RING
    groups = min(chunk // ROWS, copies)
    piece = (chunk // groups, vocab // (copies // groups))
    line = max(1, copies // 8)
    anywhere, vmem = pl.BlockSpec(memory_space=pl.ANY), pl.BlockSpec(memory_space=pltpu.VMEM)
    dma = pltpu.SemaphoreType.DMA
    return pl.pallas_call(
        functools.partial(kernel, copies, shards),
        out_shape=(
            jax.ShapeDtypeStruct((1, depth // shards), F32),
            jax.ShapeDtypeStruct((1, share), F32),
        ),
        in_specs=[anywhere] * 5,
        out_specs=(vmem, vmem),
        scratch_shapes=[
            pltpu.VMEM((depth, vocab), BF16),
            pltpu.VMEM((vocab, depth), BF16),
            pltpu.VMEM((shards, share, depth), BF16),
            pltpu.VMEM((1, depth), F32),
            pltpu.VMEM((tokens // LANES, LANES), jnp.int32),
            pltpu.SMEM((copies,), jnp.int32),
            pltpu.VMEM((tokens, depth), F32),
            pltpu.VMEM((tokens, depth), BF16),
            pltpu.VMEM((tokens, vocab), F32),
            pltpu.VMEM((tokens, vocab), BF16),
            pltpu.VMEM((tokens, LANES), F32),
            pltpu.VMEM((tokens, LANES), jnp.int32),
            pltpu.VMEM((tokens, LANES), F32),
            pltpu.VMEM((LANES, LANES), F32),
            pltpu.VMEM((1, depth), F32),
            pltpu.VMEM((1, 3 * tokens), F32),
            pltpu.VMEM((RING, 1, 3 * tokens), F32),
            pltpu.VMEM((1, 3 * tokens), F32),
            pltpu.VMEM((RING, 1, 3 * tokens), F32),
            pltpu.VMEM((1, 2 * tokens), F32),
            pltpu.VMEM((1, 2 * tokens), F32),
            pltpu.VMEM((line, 1, 2 * tokens), F32),
            pltpu.VMEM((copies // line, line, 1, 2 * tokens), F32),
            pltpu.VMEM((shards, 1, 2 * LANES), F32),
            pltpu.VMEM((shards, 1, 2 * LANES), F32),
            pltpu.VMEM((CHUNKS, copies) + piece, BF16),
        ]
        + [pltpu.VMEM((copies,) + piece, BF16)] * CHUNKS
        + [pltpu.VMEM((CHUNKS, copies) + piece, BF16)] * 2
        + [
            pltpu.SemaphoreType.REGULAR,
            dma((5,)),
            dma((2 * 3,)),
            dma((2 * 3,)),
            dma((2 * CHUNKS * 3,)),
            dma((2 * CHUNKS * 3,)),
        ]
        + [dma((1,))] * 10
        + [dma((CHUNKS,))] * 4,
        compiler_params=pltpu.CompilerParams(
            collective_id=0, has_side_effects=True, vmem_limit_bytes=56 * 1024 * 1024
        ),
        cost_estimate=pl.CostEstimate(
            flops=4 * tokens * depth * vocab,
            bytes_accessed=2 * depth * vocab,
            transcendentals=4 * tokens * vocab,
        ),
    )(hidden[0], gain, head_weight[0], targets.reshape(-1, LANES), partner)


def solution(mesh):
    in_specs = (P("copy", "fsdp", None), P("copy", None), P("copy", None, "fsdp"), P(), P())
    out_specs = (P("copy", "fsdp"), P("copy", "fsdp"))
    return jax.shard_map(
        functools.partial(per_device, mesh.shape["copy"], mesh.shape["fsdp"]),
        mesh=mesh, in_specs=in_specs, out_specs=out_specs, check_vma=False,
    )
```
